32 devices in a mesh: circ: 4 (over z), mer: 8 (over y, x, core).
Axes of the slice: x: 2, y: 2, z: 4, core: 2. Of those that a mesh axis runs over, the one named last changes fastest.
Arguments:
- adjoint: float32 [6, 8, 2048], P(None, 'circ', 'mer'), may hold values from -6 to 6
- mode_fields: float32 [3, 6, 8, 2048], P(None, None, 'circ'), may hold values from -6 to 6
- node_slot: int32 [2048], replicated, may hold values from 0 to 2047, as said below
- thickness: float32 [8, 2048], P('circ'), may hold values from 0.5 to 1.5
- weld_land: int32 [8, 2048], P('circ'), may hold values 0 or 1
- panel_spans: int32 [4, 8], P('circ'), may hold values from 1 to 768, 2048 in all within a row
- load_factor: float32 [], replicated, may hold values from 0.5 to 1.5
- membrane: float32 [24, 24], replicated, may hold values from -1.25 to 1.25
- bending: float32 [24, 24], replicated, may hold values from -0.4375 to 0.4375
- geometric: float32 [3, 24, 24], replicated, may hold values from -1.25 to 1.25
- stress_map: float32 [3, 24], replicated, may hold values from -1.25 to 1.25
Outputs:
- adjoint_load: float32 [6, 8, 2048], P(None, 'circ', 'mer')
- thickness_grad: float32 [8, 6144], P('circ', 'mer')
The draws below stay inside these ranges and needn't reach their ends.
Inputs may be any that keep to these rules, and one draw needn't show every extreme that they name: A permutation of the node positions; node_slot[j] // 256 equals j modulo 2048 // 256. `panel_spans`: each row sums to 2048 and its largest entry is 768.
All inputs are finite; a program needn't handle non-finite values. No bound on the sum of `weld_land` on one device may be relied on, other than what follows from the above.
Results may differ from the reference program's by a relative error of at most 0.0003.
Values sent between devices are 32-bit elements; how exact they have to be, the bound alone decides.
A program may use at most 128 MiB of HBM per device.

```python
import math
import jax
import jax.numpy as jnp
import numpy as np
from jax import lax

DOF = 6
CR = 2
MERN = 256
NRING = 8
MT = 2048
MOST = 768
N_CIRC = 4
N_MER = 8


def draw_node_slot(key, part):
    groups = MT // MERN
    positions = jnp.arange(MT, dtype=jnp.int32)
    owners = positions % groups
    within = positions // groups
    keys = jax.random.split(jax.random.fold_in(key, 7), groups)
    orders = jax.vmap(lambda single: jax.random.permutation(single, MERN))(keys).astype(jnp.int32)
    return (owners * MERN + orders[owners, within]).astype(jnp.int32)


def place_ends(result, stream_key, least, high):
    longest = result.shape.index(max(result.shape))
    spots = []
    for shift in (0, 1):
        where = [jax.random.randint(jax.random.fold_in(stream_key, axis), (), 0, length) for axis, length in enumerate(result.shape)]
        where[longest] = (where[longest] + shift) % result.shape[longest]
        spots.append(tuple(where))
    return result.at[spots[0]].set(least).at[spots[1]].set(high)


def steps_of(stream_key, extent, cuts, least, high):
    gain = 1.0
    for position, parts in cuts:
        heights = jax.random.uniform(jax.random.fold_in(jax.random.fold_in(stream_key, 6), position), (parts,), jnp.float32, least / len(cuts), high / len(cuts))
        gain = gain * jnp.repeat(jnp.exp(heights), extent[position] // parts).reshape((-1,) + (1,) * (len(extent) - 1 - position))
    return gain


def split_up(amount, total, reach, lean):
    portions = [(1 << 20) // math.isqrt(standing ** lean) + 1 for standing in range(2, amount + 1)]
    surplus, holding = total - reach - (amount - 1), [1] * (amount - 1)
    while surplus > 0:
        movable = [i for i in range(amount - 1) if holding[i] < reach]
        mass, budget = sum([portions[i] for i in movable]), surplus
        for i in movable:
            more = min(reach - holding[i], max(1, budget * portions[i] // mass), surplus)
            holding[i] = holding[i] + more
            surplus = surplus - more
    return np.array([reach] + holding)


def ragged(key, amount, total, limit, skew):
    if amount == 2:
        one = jax.random.randint(key, (), max(1, total - limit), min(limit, total - 1) + 1)
        return jnp.stack([one, total - one])
    tallies = jnp.asarray(split_up(amount, total, limit, skew), jnp.int32)
    twos = (amount - 1) // 2
    source_of, sink = tallies[1:1 + 2 * twos:2], tallies[2:2 + 2 * twos:2]
    slack = jnp.minimum(source_of - 1, limit - sink)
    passed = jax.random.randint(jax.random.fold_in(key, 1), (twos,), 0, 1 << 20) % (slack + 1)
    tallies = tallies.at[1:1 + 2 * twos:2].set(source_of - passed).at[2:2 + 2 * twos:2].set(sink + passed)
    return tallies[jax.random.permutation(jax.random.fold_in(key, 2), amount)]


def noise(key, dims, spread, limit, cuts=(), kind=jnp.bfloat16):
    result = spread * jax.random.normal(key, dims, jnp.float32)
    if cuts:
        result = result * steps_of(key, dims, cuts, -0.22, 0.18)
    return jnp.clip(result, -limit, limit).astype(kind)


def setup_inputs(seed: int = 0) -> dict:
    streams_of = jax.random.split(jax.random.key(seed), 12)
    adjoint = noise(streams_of[0], (DOF, NRING, MT), 1.0, 6.0, ((1, 4), (2, 8)), jnp.float32)
    mode_fields = noise(streams_of[1], (3, DOF, NRING, MT), 1.0, 6.0, ((2, 4),), jnp.float32)
    node_slot = draw_node_slot(jax.random.fold_in(streams_of[11], 71), 0)
    thickness = jnp.clip(jnp.exp(math.log(1.5) - 1.0986123 * jax.random.uniform(streams_of[3], (NRING, MT), jnp.float32) ** steps_of(streams_of[3], (NRING, MT), ((0, 4),), -0.2, 0.2)), 0.5, 1.5)
    weld_land = place_ends((jax.random.randint(streams_of[4], (NRING, MT), 0, 4) < 1).astype(jnp.int32), jax.random.fold_in(streams_of[4], 1), 0, 1)
    panel_spans = jax.vmap(lambda own: ragged(own, N_MER, MT, MOST, 2))(jax.random.split(streams_of[5], N_CIRC)).reshape((N_CIRC, N_MER)).astype(jnp.int32)
    load_factor = jnp.clip(jax.random.uniform(streams_of[6], (), jnp.float32, 0.5, 1.5), 0.5, 1.5)
    membrane = noise(streams_of[7], (24, 24), 24 ** -0.5, 1.25, (), jnp.float32)
    bending = noise(streams_of[8], (24, 24), 216 ** -0.5, 0.4375, (), jnp.float32)
    geometric = noise(streams_of[9], (3, 24, 24), 24 ** -0.5, 1.25, (), jnp.float32)
    stress_map = noise(streams_of[10], (3, 24), 24 ** -0.5, 1.25, (), jnp.float32)
    return dict(adjoint=adjoint, mode_fields=mode_fields, node_slot=node_slot, thickness=thickness, weld_land=weld_land, panel_spans=panel_spans, load_factor=load_factor, membrane=membrane, bending=bending, geometric=geometric, stress_map=stress_map)


highest = lax.Precision.HIGHEST


def element_terms(mode_vectors, adjoint_vectors, thick_rows, weld_rows, load_factor, membrane, bending, geometric, stress_map):
    land_growth = 1.0 + 0.5 * weld_rows
    thick_eff = thick_rows * land_growth
    membrane_part = jnp.einsum("ab,fbe->fae", membrane, mode_vectors, precision=highest)
    bending_part = jnp.einsum("ab,fbe->fae", bending, mode_vectors, precision=highest)
    tangent = membrane_part + 3.0 * thick_eff ** 2 * bending_part
    stiffness = jnp.sum(mode_vectors[0] * tangent[0] + mode_vectors[1] * tangent[1], axis=0)
    adjoint_term = jnp.sum(adjoint_vectors * tangent[2], axis=0)
    stress = jnp.dot(stress_map, mode_vectors[2], precision=highest)
    geometric_part = jnp.einsum("sab,kbe->ksae", geometric, mode_vectors[:2], precision=highest)
    pair_terms = jnp.sum(mode_vectors[:2, None] * geometric_part, axis=(0, 2))
    gradient = land_growth * (stiffness - load_factor * jnp.sum(stress * pair_terms, axis=0) - adjoint_term)
    load_rows = load_factor * thick_eff * jnp.dot(stress_map.T, pair_terms, precision=highest)
    return gradient, load_rows


def corners(field, cycle_axis, cycle_index, slot_here, slot_next):
    lower_cycle = lax.dynamic_index_in_dim(field, cycle_index, cycle_axis, keepdims=False)
    upper_cycle = lax.dynamic_index_in_dim(field, (cycle_index + 1) % NRING, cycle_axis, keepdims=False)
    corner_list = [jnp.take(lower_cycle, slot_here, axis=-1), jnp.take(upper_cycle, slot_here, axis=-1),
                   jnp.take(upper_cycle, slot_next, axis=-1), jnp.take(lower_cycle, slot_next, axis=-1)]
    return jnp.stack(corner_list, axis=-3)


def reference(adjoint, mode_fields, node_slot, thickness, weld_land, panel_spans, load_factor, membrane, bending, geometric, stress_map):
    slot_next = jnp.roll(node_slot, -1)

    def visit_cycle(accumulated, cycle_index):
        mode_vectors = corners(mode_fields, 2, cycle_index, node_slot, slot_next).reshape(3, 24, MT)
        adjoint_vectors = corners(adjoint, 1, cycle_index, node_slot, slot_next).reshape(24, MT)
        thick_rows = lax.dynamic_index_in_dim(thickness, cycle_index, 0, keepdims=False)
        weld_rows = lax.dynamic_index_in_dim(weld_land, cycle_index, 0, keepdims=False).astype(jnp.float32)
        gradient, load_rows = element_terms(mode_vectors, adjoint_vectors, thick_rows, weld_rows, load_factor, membrane, bending, geometric, stress_map)
        load_rows = load_rows.reshape(4, 6, MT)
        next_cycle = (cycle_index + 1) % NRING
        accumulated = accumulated.at[:, cycle_index, node_slot].add(load_rows[0])
        accumulated = accumulated.at[:, next_cycle, node_slot].add(load_rows[1])
        accumulated = accumulated.at[:, next_cycle, slot_next].add(load_rows[2])
        accumulated = accumulated.at[:, cycle_index, slot_next].add(load_rows[3])
        return accumulated, gradient

    adjoint_load, gradient_full = lax.scan(visit_cycle, jnp.zeros((6, NRING, MT), jnp.float32), jnp.arange(NRING, dtype=jnp.int32))
    span_ends = jnp.cumsum(panel_spans, axis=1).astype(jnp.int32)
    span_starts = (span_ends - panel_spans).astype(jnp.int32)
    positions = jnp.arange(MOST, dtype=jnp.int32)
    validity = positions[None, None, :] < panel_spans[:, :, None]
    columns = jnp.where(validity, span_starts[:, :, None] + positions[None, None, :], 0).astype(jnp.int32)
    panels = gradient_full.reshape(N_CIRC, CR, MT)

    def pick_panel(panel_rows, panel_columns):
        return jnp.take(panel_rows, panel_columns.reshape(-1), axis=1).reshape(CR, N_MER, MOST)

    picked = jax.vmap(pick_panel)(panels, columns)
    picked = picked * validity[:, None, :, :].astype(jnp.float32)
    thickness_grad = picked.reshape(NRING, N_MER * MOST)
    return adjoint_load, thickness_grad
```

```python
import functools
import jax
import jax.numpy as jnp
from jax import lax
from jax.experimental import pallas as pl
from jax.experimental.pallas import tpu as pltpu
from jax.sharding import PartitionSpec as P

MOST = 768
LANES = 128
WIDE = 256


def lane_gather(x, index):
    return jnp.take_along_axis(x, index, axis=1, mode="promise_in_bounds")


def split(x):
    high = x.astype(jnp.bfloat16).astype(jnp.float32)
    return high, x - high


def gather_wide(block, low_index, in_low):
    left = lane_gather(block[:, :LANES], low_index)
    right = lane_gather(block[:, LANES:], low_index)
    return jnp.where(in_low, left, right)


def iota(shape, axis):
    return lax.broadcasted_iota(jnp.int32, shape, axis)


def untangle(turned, column, positions, groups, stride=1):
    width = LANES // groups
    tile = (positions // width) * stride + column
    within = positions % width
    parts = []
    for eight in range(groups // 8):
        total = None
        for q in range(width):
            base = groups * q + 8 * eight
            picked = lane_gather(turned[base : base + 8, :], tile)
            total = picked if total is None else jnp.where(within == q, picked, total)
        parts.append(total)
    return parts


def down(x):
    return jnp.sum(x, axis=0, keepdims=True)


def stack_corners(lower_here, upper_here, upper_next, lower_next):
    return jnp.concatenate([lower_here, upper_here, upper_next, lower_next], axis=0)


def triple(v):
    high, low = split(v)
    return jnp.concatenate([high, high, low], axis=0)


def mm(a, b):
    return jnp.dot(a, b, preferred_element_type=jnp.float32)


def local_kernel(
    groups, tiles, slot_ref, span_ref, factor_ref, thick_ref, weld_ref, nodes_ref, mats_ref, map_ref,
    load_ref, carry_ref, grad_ref,
    index_ref, teff_ref, window_ref, near_ref, xy_ref,
):
    member = lax.axis_index("mer")
    factor = factor_ref[0]
    start = jnp.int32(0)
    count = jnp.int32(0)
    for g in range(groups):
        start = start + jnp.where(g < member, span_ref[0, g], 0)
        count = count + jnp.where(g == member, span_ref[0, g], 0)
    first = start // groups
    lane = iota((8, LANES), 1)

    pad = jnp.zeros((LANES - tiles, LANES), jnp.int32)
    slots = jnp.concatenate([slot_ref[...], pad], axis=0) % WIDE
    slots_t = slots.astype(jnp.float32).T.astype(jnp.int32)
    for half in range(2):
        for e, part in enumerate(untangle(slots_t, 0, lane + half * LANES, groups)):
            index_ref[8 * e : 8 * e + 8, half * LANES : (half + 1) * LANES] = part
    shifted = untangle(slots_t, 0, (first + lane) % WIDE, groups)

    growth = 1.0 + 0.5 * weld_ref[...].astype(jnp.float32)
    effective = thick_ref[...] * growth
    for cycle in range(2):
        rows = [effective[cycle : cycle + 1, t * LANES : (t + 1) * LANES] for t in range(tiles)]
        natural = jnp.concatenate(rows + [jnp.zeros((LANES - tiles, LANES), jnp.float32)], axis=0)
        natural_t = natural.T
        for half in range(2):
            for e, part in enumerate(untangle(natural_t, 0, lane + half * LANES, groups)):
                teff_ref[cycle, 8 * e : 8 * e + 8, half * LANES : (half + 1) * LANES] = part

    a_high, a_low = split(mats_ref[...])
    mats = jnp.concatenate([a_high, a_low, a_high], axis=1)

    owners, rows_of = [], []
    for d in (-1, 0, 1):
        owner = lax.rem(member + d + groups, groups)
        row = index_ref[pl.ds(owner, 1), :]
        if d == -1:
            row = jnp.where(member == 0, pltpu.roll(row, 1, 1), row)
        if d == 1:
            row = jnp.where(member == groups - 1, pltpu.roll(row, WIDE - 1, 1), row)
        owners.append(owner)
        rows_of.append(row)
    for d in range(3):
        base = pl.multiple_of(owners[d] * WIDE, WIDE)
        wide = jnp.broadcast_to(rows_of[d], (8, WIDE))
        for half in range(2):
            index = wide[:, half * LANES : (half + 1) * LANES]
            low, in_low = index % LANES, index < LANES
            for q in range(3):
                for f in range(2):
                    block = nodes_ref[q, 8 * f : 8 * f + 8, pl.ds(base, WIDE)]
                    near_ref[q, 8 * f : 8 * f + 8, d * WIDE + half * LANES : d * WIDE + (half + 1) * LANES] = (
                        gather_wide(block, low, in_low)
                    )
    loads = [jnp.zeros((8, WIDE), jnp.float32) for _ in range(3)]
    for r in range(2):
        pair = [0.0, 0.0, 0.0]
        for f in range(2):
            rows = slice(8 * f, 8 * f + 8)
            v = stack_corners(
                near_ref[r, rows, : 2 * WIDE],
                near_ref[r + 1, rows, : 2 * WIDE],
                near_ref[r + 1, rows, WIDE:],
                near_ref[r, rows, WIDE:],
            )
            product = mm(mats[64:160], triple(v))
            for s in range(3):
                pair[s] = pair[s] + down(v * product[32 * s : 32 * s + 32])
        spread = 0.0
        for s in range(3):
            spread = spread + map_ref[:, s : s + 1] * pair[s]
        behind = lax.rem(member + groups - 1, groups)
        te_here = teff_ref[r, pl.ds(member, 1), :]
        te_behind = teff_ref[r, pl.ds(behind, 1), :]
        te_behind = jnp.where(member == 0, pltpu.roll(te_behind, 1, 1), te_behind)
        from_behind_ = spread[:, :WIDE] * (factor * te_behind)
        from_here = spread[:, WIDE:] * (factor * te_here)
        loads[r] = loads[r] + from_here[0:8] + from_behind_[24:32]
        loads[r + 1] = loads[r + 1] + from_here[8:16] + from_behind_[16:24]
    values = jnp.concatenate(loads, axis=0)
    high, rest = split(values)
    middle, low3 = split(rest)
    place = (iota((WIDE, WIDE), 0) == jnp.broadcast_to(rows_of[1], (WIDE, WIDE))).astype(jnp.float32)
    placed = lax.dot_general(
        jnp.concatenate([high, middle, low3], axis=0), place, (((1,), (1,)), ((), ())),
        preferred_element_type=jnp.float32,
    )
    placed = placed[0:24] + placed[24:48] + placed[48:72]
    load_ref[0] = placed[0:8]
    load_ref[1] = placed[8:16]
    carry_ref[...] = placed[16:24]

    for o in range(groups):
        index = jnp.broadcast_to(shifted[o // 8][o % 8 : o % 8 + 1, :], (8, LANES))
        low, in_low = index % LANES, index < LANES
        for q in range(3):
            for f in range(4):
                block = nodes_ref[q, 8 * f : 8 * f + 8, o * WIDE : (o + 1) * WIDE]
                got = gather_wide(block, low, in_low)
                window_ref[q, 8 * f : 8 * f + 8, o * LANES : (o + 1) * LANES] = got
                if o == 0:
                    window_ref[q, 8 * f : 8 * f + 8, groups * LANES : (groups + 1) * LANES] = pltpu.roll(
                        got, LANES - 1, 1
                    )
    size = 8 * LANES
    for r in range(2):
        for part in range(groups // 8):
            here = slice(part * size, (part + 1) * size)
            after = slice(part * size + LANES, (part + 1) * size + LANES)

            def corner(f):
                rows = slice(8 * f, 8 * f + 8)
                return stack_corners(
                    window_ref[r, rows, here],
                    window_ref[r + 1, rows, here],
                    window_ref[r + 1, rows, after],
                    window_ref[r, rows, after],
                )

            quad = [0.0] * 5
            for f in range(2):
                v = corner(f)
                product = mm(mats, triple(v))[:160]
                for s in range(5):
                    quad[s] = quad[s] + v * product[32 * s : 32 * s + 32]
            u, a = corner(2), corner(3)
            u_three = triple(u)
            tangent = mm(mats[0:64], u_three)
            stress = mm(mats[160:168], u_three)
            geometric = 0.0
            for s in range(3):
                geometric = geometric + stress[s : s + 1] * down(quad[2 + s])
            x = down(quad[0] - a * tangent[0:32]) - factor * geometric
            y = down(quad[1] - a * tangent[32:64])
            for o in range(8):
                cut = slice(o * LANES, (o + 1) * LANES)
                xy_ref[2 * r, 8 * part + o : 8 * part + o + 1, :] = x[:, cut]
                xy_ref[2 * r + 1, 8 * part + o : 8 * part + o + 1, :] = y[:, cut]

    width = thick_ref.shape[1]
    back = lax.rem(width - start, width)
    te_span = pltpu.roll(effective, back, 1)[:, :MOST]
    growth_span = pltpu.roll(growth, back, 1)[:, :MOST]
    offset = start - first * groups
    sub = iota((8, LANES), 0)
    for b in range(MOST // LANES):
        n = lane + (b * LANES + offset)
        o_of, k_of = n % groups, n // groups
        cut = slice(b * LANES, (b + 1) * LANES)
        keep = lane[0:1] + b * LANES < count
        for r in range(2):
            both = []
            for z in range(2):
                total = 0.0
                for e in range(groups // 8):
                    picked = lane_gather(xy_ref[2 * r + z, 8 * e : 8 * e + 8, :], k_of)
                    total = total + jnp.sum(jnp.where(o_of == sub + 8 * e, picked, 0.0), axis=0, keepdims=True)
                both.append(total)
            te = te_span[r : r + 1, cut]
            g = growth_span[r : r + 1, cut] * (both[0] + 3.0 * te * te * both[1])
            grad_ref[r : r + 1, cut] = jnp.where(keep, g, 0.0)


def padded_mats(membrane, bending, geometric, stress_map):
    square = jnp.concatenate([membrane[None], bending[None], geometric], axis=0).reshape(5, 4, 6, 4, 6)
    square = jnp.pad(square, ((0, 0), (0, 0), (0, 2), (0, 0), (0, 2))).reshape(160, 32)
    rows = jnp.pad(stress_map.reshape(3, 4, 6), ((0, 5), (0, 0), (0, 2))).reshape(8, 32)
    return jnp.concatenate([square, rows], axis=0), rows.T


def on_device(
    adjoint, mode_fields, node_slot, thickness, weld_land, panel_spans, load_factor,
    membrane, bending, geometric, stress_map,
):
    column_width = mode_fields.shape[3]
    groups = lax.axis_size("mer")
    rings = lax.axis_size("circ")
    tiles = column_width // LANES
    adj_column = lax.all_gather(adjoint, "mer", axis=2, tiled=True)
    whole = jnp.concatenate([mode_fields, adj_column[None]], axis=0)
    whole = jnp.pad(jnp.transpose(whole, (2, 0, 1, 3)), ((0, 0), (0, 0), (0, 2), (0, 0))).reshape(2, 32, column_width)
    rim = lax.ppermute(whole[:1], "circ", [((i + 1) % rings, i) for i in range(rings)])
    nodes = jnp.concatenate([whole, rim], axis=0)
    mats, map_t = padded_mats(membrane, bending, geometric, stress_map)
    vmem = pl.BlockSpec(memory_space=pltpu.VMEM)
    smem = pl.BlockSpec(memory_space=pltpu.SMEM)
    load, carry, grad = pl.pallas_call(
        functools.partial(local_kernel, groups, tiles),
        out_shape=(
            jax.ShapeDtypeStruct((2, 8, WIDE), jnp.float32),
            jax.ShapeDtypeStruct((8, WIDE), jnp.float32),
            jax.ShapeDtypeStruct((2, MOST), jnp.float32),
        ),
        in_specs=[vmem, smem, smem, vmem, vmem, vmem, vmem, vmem],
        out_specs=(vmem, vmem, vmem),
        scratch_shapes=[
            pltpu.VMEM((groups, WIDE), jnp.int32),
            pltpu.VMEM((2, groups, WIDE), jnp.float32),
            pltpu.VMEM((3, 32, (groups + 1) * LANES), jnp.float32),
            pltpu.VMEM((3, 16, 3 * WIDE), jnp.float32),
            pltpu.VMEM((4, groups, LANES), jnp.float32),
        ],
        compiler_params=pltpu.CompilerParams(vmem_limit_bytes=32 * 1024 * 1024),
    )(
        node_slot.reshape(tiles, LANES), panel_spans, load_factor.reshape(1), thickness, weld_land,
        nodes, mats, map_t,
    )
    carried = lax.ppermute(carry, "circ", [(i, (i + 1) % rings) for i in range(rings)])
    load = load.at[0].add(carried)
    adjoint_load = jnp.transpose(load[:, :6], (1, 0, 2))
    return (adjoint_load, grad)


def solution(mesh):
    return jax.shard_map(
        on_device,
        mesh=mesh,
        in_specs=(
            P(None, "circ", "mer"),
            P(None, None, "circ", None),
            P(),
            P("circ", None),
            P("circ", None),
            P("circ", None),
            P(),
            P(),
            P(),
            P(),
            P(),
        ),
        out_specs=(P(None, "circ", "mer"), P("circ", "mer")),
        check_vma=False,
    )
```

```python
import functools
import jax
import jax.numpy as jnp
from jax import lax
from jax.experimental import pallas as pl
from jax.experimental.pallas import tpu as pltpu
from jax.sharding import PartitionSpec as P

MOST = 768
LANES = 128
WIDE = 256


def lane_gather(x, index):
    return jnp.take_along_axis(x, index, axis=1, mode="promise_in_bounds")


def split(x):
    high = x.astype(jnp.bfloat16).astype(jnp.float32)
    return high, x - high


def gather_wide(block, low_index, in_low):
    left = lane_gather(block[:, :LANES], low_index)
    right = lane_gather(block[:, LANES:], low_index)
    return jnp.where(in_low, left, right)


def iota(shape, axis):
    return lax.broadcasted_iota(jnp.int32, shape, axis)


def untangle(turned, column, positions, groups, stride=1):
    width = LANES // groups
    tile = (positions // width) * stride + column
    within = positions % width
    parts = []
    for eight in range(groups // 8):
        total = None
        for q in range(width):
            base = groups * q + 8 * eight
            picked = lane_gather(turned[base : base + 8, :], tile)
            total = picked if total is None else jnp.where(within == q, picked, total)
        parts.append(total)
    return parts


def down(x):
    return jnp.sum(x, axis=0, keepdims=True)


def stack_corners(lower_here, upper_here, upper_next, lower_next):
    return jnp.concatenate([lower_here, upper_here, upper_next, lower_next], axis=0)


def triple(v):
    high, low = split(v)
    return jnp.concatenate([high, high, low], axis=0)


def nt(a, b):
    return lax.dot_general(a, b, (((1,), (1,)), ((), ())), preferred_element_type=jnp.float32)


def mm(a, b):
    return jnp.dot(a, b, preferred_element_type=jnp.float32)


def prepared_mats(membrane, bending, geometric, stress_map):
    stress = jnp.concatenate([stress_map, jnp.zeros((5, 24), jnp.float32)], axis=0)
    stacked = jnp.concatenate([membrane, bending, geometric[0], geometric[1], geometric[2], stress], axis=0)
    high, low = split(stacked)
    i, j = iota((24, 96), 0), iota((24, 96), 1)
    lands = (j % 8 < 6) & (i == 6 * (j % 32 // 8) + j % 8)
    from_low = j // 32 == 1
    put_high = jnp.where(lands & jnp.logical_not(from_low), 1.0, 0.0)
    put_low = jnp.where(lands & from_low, 1.0, 0.0)
    wide = mm(high, put_high) + mm(low, put_low)
    row, source = iota((168, 128), 0), iota((168, 128), 1)
    within = row % 32
    square = (row < 160) & (within % 8 < 6) & (source == 24 * (row // 32) + 6 * (within // 8) + within % 8)
    plain = (row >= 160) & (source == row - 40)
    mats = mm(jnp.where(square | plain, 1.0, 0.0), wide)
    k, c = iota((32, 24), 0), iota((32, 24), 1)
    pick = jnp.where((k % 8 < 6) & (c == 6 * (k // 8) + k % 8), 1.0, 0.0)
    s_high, rest = split(stress)
    s_mid, s_low = split(rest)
    return mats, nt(pick, s_high) + nt(pick, s_mid) + nt(pick, s_low)


def whole_kernel(
    groups, rings, tiles, slot_far, span_far, factor_far, thick_far, weld_far, mode_far, adj_far,
    membrane_far, bending_far, geometric_far, stress_far,
    load_ref, grad_ref,
    nodes_ref, index_ref, teff_ref, window_ref, near_ref, xy_ref, carry_out, carry_in,
    plane_send, plane_recv, adj_send, adj_recv, rim_send, rim_recv, fwd_send, fwd_recv, carry_send, carry_recv,
    slot_ref, span_ref, factor_ref, thick_ref, weld_ref, mode_ref, adj_ref,
    membrane_ref, bending_ref, geometric_ref, stress_ref, input_sem,
):
    mesh_id = pl.DeviceIdType.MESH
    far = (mode_far, adj_far, slot_far, span_far, factor_far, thick_far, weld_far,
           membrane_far, bending_far, geometric_far, stress_far)
    close = (mode_ref, adj_ref, slot_ref, span_ref, factor_ref, thick_ref, weld_ref,
             membrane_ref, bending_ref, geometric_ref, stress_ref)
    inputs = [pltpu.make_async_copy(a, b, input_sem.at[n]) for n, (a, b) in enumerate(zip(far, close))]
    for copy in inputs:
        copy.start()
    half_groups = groups // 2
    ring, member = lax.axis_index("circ"), lax.axis_index("mer")
    below, above = lax.rem(ring + rings - 1, rings), lax.rem(ring + 1, rings)
    parity, pair_of = member % 2, member // 2
    same = [2 * lax.rem(pair_of + i, half_groups) + parity for i in range(half_groups)]

    barrier = pltpu.get_barrier_semaphore()
    for d in range(1, groups):
        pl.semaphore_signal(barrier, inc=1, device_id=(ring, lax.rem(member + d, groups)), device_id_type=mesh_id)
    for i in range(half_groups):
        pl.semaphore_signal(barrier, inc=1, device_id=(below, same[i]), device_id_type=mesh_id)
        pl.semaphore_signal(barrier, inc=1, device_id=(above, same[i]), device_id_type=mesh_id)

    for copy in inputs[:2]:
        copy.wait()
    empty = jnp.zeros((2, LANES), jnp.float32)
    own = pl.multiple_of(member * WIDE, WIDE)
    stride = 2 * tiles
    for q in range(2):
        for f in range(3):
            for t in range(tiles):
                six = mode_ref[pl.ds(f * 6 * stride + 2 * t + q, 6, stride=stride), :]
                nodes_ref[q, 8 * f : 8 * f + 8, t * LANES : (t + 1) * LANES] = jnp.concatenate([six, empty], axis=0)
        for t in range(2):
            six = adj_ref[pl.ds(2 * t + q, 6, stride=4), :]
            nodes_ref[q, 24:32, pl.ds(own + t * LANES, LANES)] = jnp.concatenate([six, empty], axis=0)
    pl.semaphore_wait(barrier, groups - 1 + 2 * half_groups)

    def block_of(owner):
        return pl.ds(pl.multiple_of(owner * WIDE, WIDE), WIDE)

    rims, adjs, planes, forwards = [], [], [], []
    owners_same = [2 * lax.rem(pair_of + half_groups - i, half_groups) + parity for i in range(half_groups)]
    for i in range(half_groups):
        adjs.append(pltpu.make_async_remote_copy(
            src_ref=nodes_ref.at[0, pl.ds(24, 8), block_of(member)],
            dst_ref=nodes_ref.at[2, pl.ds(24, 8), block_of(member)],
            send_sem=adj_send.at[i], recv_sem=adj_recv.at[i],
            device_id=(below, same[i]), device_id_type=mesh_id))
        rims.append(pltpu.make_async_remote_copy(
            src_ref=nodes_ref.at[0, pl.ds(0, 24), block_of(owners_same[i])],
            dst_ref=nodes_ref.at[2, pl.ds(0, 24), block_of(owners_same[i])],
            send_sem=rim_send.at[i], recv_sem=rim_recv.at[i],
            device_id=(below, member), device_id_type=mesh_id))
        adjs[i].start()
        rims[i].start()
    for d in range(1, groups):
        planes.append(pltpu.make_async_remote_copy(
            src_ref=nodes_ref.at[pl.ds(0, 2), pl.ds(24, 8), block_of(member)],
            dst_ref=nodes_ref.at[pl.ds(0, 2), pl.ds(24, 8), block_of(member)],
            send_sem=plane_send.at[d], recv_sem=plane_recv.at[d],
            device_id=(ring, lax.rem(member + d, groups)), device_id_type=mesh_id))
        planes[-1].start()
    for i in range(half_groups):
        forwards.append(pltpu.make_async_remote_copy(
            src_ref=nodes_ref.at[2, pl.ds(0, 32), block_of(owners_same[i])],
            dst_ref=nodes_ref.at[2, pl.ds(0, 32), block_of(owners_same[i])],
            send_sem=fwd_send.at[i], recv_sem=fwd_recv.at[i],
            device_id=(ring, member + 1 - 2 * parity), device_id_type=mesh_id))

    def send_on():
        for i in range(half_groups):
            adjs[i].wait_recv()
            rims[i].wait_recv()
            forwards[i].start()

    for copy in inputs[2:]:
        copy.wait()
    factor = factor_ref[0, 0]
    start = jnp.int32(0)
    count = jnp.int32(0)
    for g in range(groups):
        start = start + jnp.where(g < member, span_ref[0, g], 0)
        count = count + jnp.where(g == member, span_ref[0, g], 0)
    first = start // groups
    lane = iota((8, LANES), 1)

    pad = jnp.zeros((LANES - tiles, LANES), jnp.int32)
    slots = jnp.concatenate([slot_ref[...], pad], axis=0) % WIDE
    slots_t = slots.astype(jnp.float32).T.astype(jnp.int32)
    for half in range(2):
        for e, part in enumerate(untangle(slots_t, 0, lane + half * LANES, groups)):
            index_ref[8 * e : 8 * e + 8, half * LANES : (half + 1) * LANES] = part
    shifted = untangle(slots_t, 0, (first + lane) % WIDE, groups)

    growth = 1.0 + 0.5 * weld_ref[...].astype(jnp.float32)
    effective = thick_ref[...] * growth
    for cycle in range(2):
        rows = [effective[cycle : cycle + 1, t * LANES : (t + 1) * LANES] for t in range(tiles)]
        natural = jnp.concatenate(rows + [jnp.zeros((LANES - tiles, LANES), jnp.float32)], axis=0)
        natural_t = natural.T
        for half in range(2):
            for e, part in enumerate(untangle(natural_t, 0, lane + half * LANES, groups)):
                teff_ref[cycle, 8 * e : 8 * e + 8, half * LANES : (half + 1) * LANES] = part

    mats, map_t = prepared_mats(membrane_ref[...], bending_ref[...], geometric_ref[...], stress_ref[...])

    owners, rows_of = [], []
    for d in (-1, 0, 1):
        owner = lax.rem(member + d + groups, groups)
        row = index_ref[pl.ds(owner, 1), :]
        if d == -1:
            row = jnp.where(member == 0, pltpu.roll(row, 1, 1), row)
        if d == 1:
            row = jnp.where(member == groups - 1, pltpu.roll(row, WIDE - 1, 1), row)
        owners.append(owner)
        rows_of.append(row)
    def gather_near(cycles):
        for d in range(3):
            base = pl.multiple_of(owners[d] * WIDE, WIDE)
            wide = jnp.broadcast_to(rows_of[d], (8, WIDE))
            for half in range(2):
                index = wide[:, half * LANES : (half + 1) * LANES]
                low, in_low = index % LANES, index < LANES
                for q in cycles:
                    for f in range(2):
                        block = nodes_ref[q, 8 * f : 8 * f + 8, pl.ds(base, WIDE)]
                        near_ref[q, 8 * f : 8 * f + 8, d * WIDE + half * LANES : d * WIDE + (half + 1) * LANES] = (
                            gather_wide(block, low, in_low)
                        )

    def cycle_loads(r):
        pair = [0.0, 0.0, 0.0]
        for f in range(2):
            rows = slice(8 * f, 8 * f + 8)
            v = stack_corners(
                near_ref[r, rows, : 2 * WIDE],
                near_ref[r + 1, rows, : 2 * WIDE],
                near_ref[r + 1, rows, WIDE:],
                near_ref[r, rows, WIDE:],
            )
            product = mm(mats[64:160], triple(v))
            for s in range(3):
                pair[s] = pair[s] + down(v * product[32 * s : 32 * s + 32])
        spread = 0.0
        for s in range(3):
            spread = spread + map_t[:, s : s + 1] * pair[s]
        behind = lax.rem(member + groups - 1, groups)
        te_here = teff_ref[r, pl.ds(member, 1), :]
        te_behind = teff_ref[r, pl.ds(behind, 1), :]
        te_behind = jnp.where(member == 0, pltpu.roll(te_behind, 1, 1), te_behind)
        from_behind_ = spread[:, :WIDE] * (factor * te_behind)
        from_here = spread[:, WIDE:] * (factor * te_here)
        loads[r] = loads[r] + from_here[0:8] + from_behind_[24:32]
        loads[r + 1] = loads[r + 1] + from_here[8:16] + from_behind_[16:24]

    def gather_window(cycles, fields):
        for o in range(groups):
            index = jnp.broadcast_to(shifted[o // 8][o % 8 : o % 8 + 1, :], (8, LANES))
            low, in_low = index % LANES, index < LANES
            for q in cycles:
                for f in fields:
                    block = nodes_ref[q, 8 * f : 8 * f + 8, o * WIDE : (o + 1) * WIDE]
                    got = gather_wide(block, low, in_low)
                    window_ref[q, 8 * f : 8 * f + 8, o * LANES : (o + 1) * LANES] = got
                    if o == 0:
                        window_ref[q, 8 * f : 8 * f + 8, groups * LANES : (groups + 1) * LANES] = pltpu.roll(
                            got, LANES - 1, 1
                        )

    size = 8 * LANES
    def elements(r):
        for part in range(groups // 8):
            here = slice(part * size, (part + 1) * size)
            after = slice(part * size + LANES, (part + 1) * size + LANES)

            def corner(f):
                rows = slice(8 * f, 8 * f + 8)
                return stack_corners(
                    window_ref[r, rows, here],
                    window_ref[r + 1, rows, here],
                    window_ref[r + 1, rows, after],
                    window_ref[r, rows, after],
                )

            quad = [0.0] * 5
            for f in range(2):
                v = corner(f)
                product = mm(mats, triple(v))[:160]
                for s in range(5):
                    quad[s] = quad[s] + v * product[32 * s : 32 * s + 32]
            u, a = corner(2), corner(3)
            u_three = triple(u)
            tangent = mm(mats[0:64], u_three)
            stress = mm(mats[160:168], u_three)
            geometric = 0.0
            for s in range(3):
                geometric = geometric + stress[s : s + 1] * down(quad[2 + s])
            x = down(quad[0] - a * tangent[0:32]) - factor * geometric
            y = down(quad[1] - a * tangent[32:64])
            for o in range(8):
                cut = slice(o * LANES, (o + 1) * LANES)
                xy_ref[2 * r, 8 * part + o : 8 * part + o + 1, :] = x[:, cut]
                xy_ref[2 * r + 1, 8 * part + o : 8 * part + o + 1, :] = y[:, cut]

    loads = [jnp.zeros((8, WIDE), jnp.float32) for _ in range(3)]
    gather_near((0, 1))
    cycle_loads(0)
    send_on()
    gather_window((0, 1), (0, 1, 2))
    for copy in planes:
        copy.wait_recv()
    gather_window((0, 1), (3,))
    elements(0)
    for copy in forwards:
        copy.wait_recv()
    gather_near((2,))
    cycle_loads(1)
    values = jnp.concatenate(loads, axis=0)
    high, rest = split(values)
    middle, low3 = split(rest)
    place = (iota((WIDE, WIDE), 0) == jnp.broadcast_to(rows_of[1], (WIDE, WIDE))).astype(jnp.float32)
    placed = lax.dot_general(
        jnp.concatenate([high, middle, low3], axis=0), place, (((1,), (1,)), ((), ())),
        preferred_element_type=jnp.float32,
    )
    placed = placed[0:24] + placed[24:48] + placed[48:72]
    carry_out[...] = placed[16:24]
    carry = pltpu.make_async_remote_copy(
        src_ref=carry_out, dst_ref=carry_in, send_sem=carry_send, recv_sem=carry_recv,
        device_id=(above, member), device_id_type=mesh_id)
    carry.start()

    gather_window((2,), (0, 1, 2, 3))
    elements(1)

    width = thick_ref.shape[1]
    back = lax.rem(width - start, width)
    te_span = pltpu.roll(effective, back, 1)[:, :MOST]
    growth_span = pltpu.roll(growth, back, 1)[:, :MOST]
    offset = start - first * groups
    sub = iota((8, LANES), 0)
    for b in range(MOST // LANES):
        n = lane + (b * LANES + offset)
        o_of, k_of = n % groups, n // groups
        cut = slice(b * LANES, (b + 1) * LANES)
        keep = lane[0:1] + b * LANES < count
        for r in range(2):
            both = []
            for z in range(2):
                total = 0.0
                for e in range(groups // 8):
                    picked = lane_gather(xy_ref[2 * r + z, 8 * e : 8 * e + 8, :], k_of)
                    total = total + jnp.sum(jnp.where(o_of == sub + 8 * e, picked, 0.0), axis=0, keepdims=True)
                both.append(total)
            te = te_span[r : r + 1, cut]
            g = growth_span[r : r + 1, cut] * (both[0] + 3.0 * te * te * both[1])
            grad_ref[r : r + 1, cut] = jnp.where(keep, g, 0.0)

    carry.wait_recv()
    load_ref[:, 0, :] = (placed[0:8] + carry_in[...])[0:6]
    load_ref[:, 1, :] = placed[8:14]
    carry.wait_send()
    for copy in rims + adjs + planes + forwards:
        copy.wait_send()


def on_device(
    adjoint, mode_fields, node_slot, thickness, weld_land, panel_spans, load_factor,
    membrane, bending, geometric, stress_map,
):
    column_width = mode_fields.shape[3]
    groups = lax.axis_size("mer")
    rings = lax.axis_size("circ")
    tiles = column_width // LANES
    mode_rows = mode_fields.reshape(3, 6, 2, tiles, LANES).transpose(0, 1, 3, 2, 4).reshape(-1, LANES)
    adj_rows = adjoint.reshape(6, 2, 2, LANES).transpose(0, 2, 1, 3).reshape(-1, LANES)
    vmem = pl.BlockSpec(memory_space=pltpu.VMEM)
    hbm = pl.BlockSpec(memory_space=pltpu.HBM)
    half_groups = groups // 2
    dma = pltpu.SemaphoreType.DMA
    return pl.pallas_call(
        functools.partial(whole_kernel, groups, rings, tiles),
        out_shape=(
            jax.ShapeDtypeStruct((6, 2, WIDE), jnp.float32),
            jax.ShapeDtypeStruct((2, MOST), jnp.float32),
        ),
        in_specs=[hbm] * 11,
        out_specs=(vmem, vmem),
        scratch_shapes=[
            pltpu.VMEM((3, 32, column_width), jnp.float32),
            pltpu.VMEM((groups, WIDE), jnp.int32),
            pltpu.VMEM((2, groups, WIDE), jnp.float32),
            pltpu.VMEM((3, 32, (groups + 1) * LANES), jnp.float32),
            pltpu.VMEM((3, 16, 3 * WIDE), jnp.float32),
            pltpu.VMEM((4, groups, LANES), jnp.float32),
            pltpu.VMEM((8, WIDE), jnp.float32),
            pltpu.VMEM((8, WIDE), jnp.float32),
            dma((groups,)), dma((groups,)),
            dma((half_groups,)), dma((half_groups,)),
            dma((half_groups,)), dma((half_groups,)),
            dma((half_groups,)), dma((half_groups,)),
            dma, dma,
            pltpu.VMEM((tiles, LANES), jnp.int32),
            pltpu.SMEM((1, groups), jnp.int32),
            pltpu.SMEM((1, 1), jnp.float32),
            pltpu.VMEM((2, column_width), jnp.float32),
            pltpu.VMEM((2, column_width), jnp.int32),
            pltpu.VMEM(mode_rows.shape, jnp.float32),
            pltpu.VMEM(adj_rows.shape, jnp.float32),
            pltpu.VMEM((24, 24), jnp.float32),
            pltpu.VMEM((24, 24), jnp.float32),
            pltpu.VMEM((3, 24, 24), jnp.float32),
            pltpu.VMEM((3, 24), jnp.float32),
            dma((11,)),
        ],
        compiler_params=pltpu.CompilerParams(
            vmem_limit_bytes=60 * 1024 * 1024, collective_id=0, has_side_effects=True
        ),
    )(
        node_slot.reshape(tiles, LANES), panel_spans, load_factor.reshape(1, 1), thickness, weld_land,
        mode_rows, adj_rows, membrane, bending, geometric, stress_map,
    )


def solution(mesh):
    return jax.shard_map(
        on_device,
        mesh=mesh,
        in_specs=(
            P(None, "circ", "mer"),
            P(None, None, "circ", None),
            P(),
            P("circ", None),
            P("circ", None),
            P("circ", None),
            P(),
            P(),
            P(),
            P(),
            P(),
        ),
        out_specs=(P(None, "circ", "mer"), P("circ", "mer")),
        check_vma=False,
    )
```

```python
import functools
import jax
import jax.numpy as jnp
from jax import lax
from jax.experimental import pallas as pl
from jax.experimental.pallas import tpu as pltpu
from jax.sharding import PartitionSpec as P

MOST = 768
LANES = 128
WIDE = 256


def lane_gather(x, index):
    return jnp.take_along_axis(x, index, axis=1, mode="promise_in_bounds")


def split(x):
    high = x.astype(jnp.bfloat16).astype(jnp.float32)
    return high, x - high


def gather_wide(block, low_index, in_low):
    left = lane_gather(block[:, :LANES], low_index)
    right = lane_gather(block[:, LANES:], low_index)
    return jnp.where(in_low, left, right)


def iota(shape, axis):
    return lax.broadcasted_iota(jnp.int32, shape, axis)


def untangle(turned, column, positions, groups, stride=1):
    width = LANES // groups
    tile = (positions // width) * stride + column
    within = positions % width
    parts = []
    for eight in range(groups // 8):
        total = None
        for q in range(width):
            base = groups * q + 8 * eight
            picked = lane_gather(turned[base : base + 8, :], tile)
            total = picked if total is None else jnp.where(within == q, picked, total)
        parts.append(total)
    return parts


def down(x):
    return jnp.sum(x, axis=0, keepdims=True)


def stack_corners(lower_here, upper_here, upper_next, lower_next):
    return jnp.concatenate([lower_here, upper_here, upper_next, lower_next], axis=0)


def triple(v):
    high, low = split(v)
    return jnp.concatenate([high, high, low], axis=0)


def nt(a, b):
    return lax.dot_general(a, b, (((1,), (1,)), ((), ())), preferred_element_type=jnp.float32)


def mm(a, b):
    return jnp.dot(a, b, preferred_element_type=jnp.float32)


def prepared_mats(membrane, bending, geometric, stress_map):
    stress = jnp.concatenate([stress_map, jnp.zeros((5, 24), jnp.float32)], axis=0)
    stacked = jnp.concatenate([membrane, bending, geometric[0], geometric[1], geometric[2], stress], axis=0)
    high, low = split(stacked)
    i, j = iota((24, 96), 0), iota((24, 96), 1)
    lands = (j % 8 < 6) & (i == 6 * (j % 32 // 8) + j % 8)
    from_low = j // 32 == 1
    put_high = jnp.where(lands & jnp.logical_not(from_low), 1.0, 0.0)
    put_low = jnp.where(lands & from_low, 1.0, 0.0)
    wide = mm(high, put_high) + mm(low, put_low)
    row, source = iota((168, 128), 0), iota((168, 128), 1)
    within = row % 32
    square = (row < 160) & (within % 8 < 6) & (source == 24 * (row // 32) + 6 * (within // 8) + within % 8)
    plain = (row >= 160) & (source == row - 40)
    mats = mm(jnp.where(square | plain, 1.0, 0.0), wide)
    k, c = iota((32, 24), 0), iota((32, 24), 1)
    pick = jnp.where((k % 8 < 6) & (c == 6 * (k // 8) + k % 8), 1.0, 0.0)
    s_high, rest = split(stress)
    s_mid, s_low = split(rest)
    return mats, nt(pick, s_high) + nt(pick, s_mid) + nt(pick, s_low)


def whole_kernel(
    groups, rings, tiles, slot_far, span_far, factor_far, thick_far, weld_far, mode_far, adj_far,
    membrane_far, bending_far, geometric_far, stress_far,
    load_ref, grad_ref,
    nodes_ref, index_ref, teff_ref, window_ref, near_ref, xy_ref, te_out, te_in,
    plane_send, plane_recv, adj_send, adj_recv, rim_send, rim_recv, fwd_send, fwd_recv, carry_send, carry_recv,
    slot_ref, span_ref, factor_ref, thick_ref, weld_ref, mode_ref, adj_ref,
    membrane_ref, bending_ref, geometric_ref, stress_ref, input_sem,
):
    mesh_id = pl.DeviceIdType.MESH
    far = (mode_far, adj_far, slot_far, span_far, factor_far, thick_far, weld_far,
           membrane_far, bending_far, geometric_far, stress_far)
    close = (mode_ref, adj_ref, slot_ref, span_ref, factor_ref, thick_ref, weld_ref,
             membrane_ref, bending_ref, geometric_ref, stress_ref)
    inputs = [pltpu.make_async_copy(a, b, input_sem.at[n]) for n, (a, b) in enumerate(zip(far, close))]
    for copy in inputs:
        copy.start()
    half_groups = groups // 2
    ring, member = lax.axis_index("circ"), lax.axis_index("mer")
    below, above = lax.rem(ring + rings - 1, rings), lax.rem(ring + 1, rings)
    parity, pair_of = member % 2, member // 2
    same = [2 * lax.rem(pair_of + i, half_groups) + parity for i in range(half_groups)]

    barrier = pltpu.get_barrier_semaphore()
    for d in range(1, groups):
        pl.semaphore_signal(barrier, inc=1, device_id=(ring, lax.rem(member + d, groups)), device_id_type=mesh_id)
    for i in range(half_groups):
        pl.semaphore_signal(barrier, inc=1, device_id=(below, same[i]), device_id_type=mesh_id)
        pl.semaphore_signal(barrier, inc=1, device_id=(above, same[i]), device_id_type=mesh_id)

    for copy in inputs[:2]:
        copy.wait()
    empty = jnp.zeros((2, LANES), jnp.float32)
    own = pl.multiple_of(member * WIDE, WIDE)
    stride = 2 * tiles
    for f in range(4):
        nodes_ref[2, f, 6:8, :] = jnp.zeros((2, tiles * LANES), jnp.float32)
    for o in range(groups):
        for q in range(2):
            nodes_ref[q, 3, 6:8, o * WIDE : (o + 1) * WIDE] = jnp.zeros((2, WIDE), jnp.float32)
    for q in range(2):
        for f in range(3):
            for t in range(tiles):
                six = mode_ref[pl.ds(f * 6 * stride + 2 * t + q, 6, stride=stride), :]
                nodes_ref[q, f, :, t * LANES : (t + 1) * LANES] = jnp.concatenate([six, empty], axis=0)
        for t in range(2):
            six = adj_ref[pl.ds(2 * t + q, 6, stride=4), :]
            nodes_ref[q, 3, 0:6, pl.ds(own + t * LANES, LANES)] = six
    pl.semaphore_wait(barrier, groups - 1 + 2 * half_groups)

    def block_of(owner):
        return pl.ds(pl.multiple_of(owner * WIDE, WIDE), WIDE)

    rims, adjs, planes, forwards = [], [], [], []
    owners_same = [2 * lax.rem(pair_of + half_groups - i, half_groups) + parity for i in range(half_groups)]
    for i in range(half_groups):
        adjs.append(pltpu.make_async_remote_copy(
            src_ref=nodes_ref.at[0, pl.ds(3, 1), pl.ds(0, 6), block_of(member)],
            dst_ref=nodes_ref.at[2, pl.ds(3, 1), pl.ds(0, 6), block_of(member)],
            send_sem=adj_send.at[i], recv_sem=adj_recv.at[i],
            device_id=(below, same[i]), device_id_type=mesh_id))
        rims.append(pltpu.make_async_remote_copy(
            src_ref=nodes_ref.at[0, pl.ds(0, 3), pl.ds(0, 6), block_of(owners_same[i])],
            dst_ref=nodes_ref.at[2, pl.ds(0, 3), pl.ds(0, 6), block_of(owners_same[i])],
            send_sem=rim_send.at[i], recv_sem=rim_recv.at[i],
            device_id=(below, member), device_id_type=mesh_id))
        adjs[i].start()
        rims[i].start()
    for d in range(1, groups):
        planes.append(pltpu.make_async_remote_copy(
            src_ref=nodes_ref.at[pl.ds(0, 2), pl.ds(3, 1), pl.ds(0, 6), block_of(member)],
            dst_ref=nodes_ref.at[pl.ds(0, 2), pl.ds(3, 1), pl.ds(0, 6), block_of(member)],
            send_sem=plane_send.at[d], recv_sem=plane_recv.at[d],
            device_id=(ring, lax.rem(member + d, groups)), device_id_type=mesh_id))
        planes[-1].start()
    for i in range(half_groups):
        forwards.append(pltpu.make_async_remote_copy(
            src_ref=nodes_ref.at[2, pl.ds(0, 4), pl.ds(0, 6), block_of(owners_same[i])],
            dst_ref=nodes_ref.at[2, pl.ds(0, 4), pl.ds(0, 6), block_of(owners_same[i])],
            send_sem=fwd_send.at[i], recv_sem=fwd_recv.at[i],
            device_id=(ring, member + 1 - 2 * parity), device_id_type=mesh_id))

    def send_on():
        for i in range(half_groups):
            adjs[i].wait_recv()
            rims[i].wait_recv()
            forwards[i].start()

    for copy in inputs[2:]:
        copy.wait()
    factor = factor_ref[0, 0]
    start = jnp.int32(0)
    count = jnp.int32(0)
    for g in range(groups):
        start = start + jnp.where(g < member, span_ref[0, g], 0)
        count = count + jnp.where(g == member, span_ref[0, g], 0)
    first = start // groups
    lane = iota((8, LANES), 1)

    pad = jnp.zeros((LANES - tiles, LANES), jnp.int32)
    slots = jnp.concatenate([slot_ref[...], pad], axis=0) % WIDE
    slots_t = slots.astype(jnp.float32).T.astype(jnp.int32)
    for half in range(2):
        for e, part in enumerate(untangle(slots_t, 0, lane + half * LANES, groups)):
            index_ref[8 * e : 8 * e + 8, half * LANES : (half + 1) * LANES] = part
    shifted = untangle(slots_t, 0, (first + lane) % WIDE, groups)

    growth = 1.0 + 0.5 * weld_ref[...].astype(jnp.float32)
    effective = thick_ref[...] * growth
    for cycle in range(2):
        rows = [effective[cycle : cycle + 1, t * LANES : (t + 1) * LANES] for t in range(tiles)]
        natural = jnp.concatenate(rows + [jnp.zeros((LANES - tiles, LANES), jnp.float32)], axis=0)
        natural_t = natural.T
        for half in range(2):
            for e, part in enumerate(untangle(natural_t, 0, lane + half * LANES, groups)):
                teff_ref[cycle, 8 * e : 8 * e + 8, half * LANES : (half + 1) * LANES] = part

    mats, map_t = prepared_mats(membrane_ref[...], bending_ref[...], geometric_ref[...], stress_ref[...])

    owners, rows_of = [], []
    for d in (-1, 0, 1):
        owner = lax.rem(member + d + groups, groups)
        row = index_ref[pl.ds(owner, 1), :]
        if d == -1:
            row = jnp.where(member == 0, pltpu.roll(row, 1, 1), row)
        if d == 1:
            row = jnp.where(member == groups - 1, pltpu.roll(row, WIDE - 1, 1), row)
        owners.append(owner)
        rows_of.append(row)
    def gather_near(cycles):
        for d in range(3):
            base = pl.multiple_of(owners[d] * WIDE, WIDE)
            wide = jnp.broadcast_to(rows_of[d], (8, WIDE))
            for half in range(2):
                index = wide[:, half * LANES : (half + 1) * LANES]
                low, in_low = index % LANES, index < LANES
                for q in cycles:
                    for f in range(2):
                        block = nodes_ref[q, f, :, pl.ds(base, WIDE)]
                        near_ref[q, 8 * f : 8 * f + 8, d * WIDE + half * LANES : d * WIDE + (half + 1) * LANES] = (
                            gather_wide(block, low, in_low)
                        )

    behind = lax.rem(member + groups - 1, groups)

    def te_of(r):
        te_behind = teff_ref[r, pl.ds(behind, 1), :]
        te_behind = jnp.where(member == 0, pltpu.roll(te_behind, 1, 1), te_behind)
        return jnp.concatenate([te_behind, teff_ref[r, pl.ds(member, 1), :]], axis=1)

    def cycle_loads(lower, upper, te):
        pair = [0.0, 0.0, 0.0]
        for f in range(2):
            rows = slice(8 * f, 8 * f + 8)
            v = stack_corners(
                near_ref[lower, rows, : 2 * WIDE],
                near_ref[upper, rows, : 2 * WIDE],
                near_ref[upper, rows, WIDE:],
                near_ref[lower, rows, WIDE:],
            )
            product = mm(mats[64:160], triple(v))
            for s in range(3):
                pair[s] = pair[s] + down(v * product[32 * s : 32 * s + 32])
        spread = 0.0
        for s in range(3):
            spread = spread + map_t[:, s : s + 1] * pair[s]
        spread = spread * (factor * te)
        return (
            spread[0:8, WIDE:] + spread[24:32, :WIDE],
            spread[8:16, WIDE:] + spread[16:24, :WIDE],
        )

    def gather_window(cycles, fields):
        for o in range(groups):
            index = jnp.broadcast_to(shifted[o // 8][o % 8 : o % 8 + 1, :], (8, LANES))
            low, in_low = index % LANES, index < LANES
            for q in cycles:
                for f in fields:
                    block = nodes_ref[q, f, :, o * WIDE : (o + 1) * WIDE]
                    got = gather_wide(block, low, in_low)
                    window_ref[q, 8 * f : 8 * f + 8, o * LANES : (o + 1) * LANES] = got
                    if o == 0:
                        window_ref[q, 8 * f : 8 * f + 8, groups * LANES : (groups + 1) * LANES] = pltpu.roll(
                            got, LANES - 1, 1
                        )

    size = 8 * LANES
    def elements(r):
        for part in range(groups // 8):
            here = slice(part * size, (part + 1) * size)
            after = slice(part * size + LANES, (part + 1) * size + LANES)

            def corner(f):
                rows = slice(8 * f, 8 * f + 8)
                return stack_corners(
                    window_ref[r, rows, here],
                    window_ref[r + 1, rows, here],
                    window_ref[r + 1, rows, after],
                    window_ref[r, rows, after],
                )

            quad = [0.0] * 5
            for f in range(2):
                v = corner(f)
                product = mm(mats, triple(v))[:160]
                for s in range(5):
                    quad[s] = quad[s] + v * product[32 * s : 32 * s + 32]
            u, a = corner(2), corner(3)
            u_three = triple(u)
            tangent = mm(mats[0:64], u_three)
            stress = mm(mats[160:168], u_three)
            geometric = 0.0
            for s in range(3):
                geometric = geometric + stress[s : s + 1] * down(quad[2 + s])
            x = down(quad[0] - a * tangent[0:32]) - factor * geometric
            y = down(quad[1] - a * tangent[32:64])
            for o in range(8):
                cut = slice(o * LANES, (o + 1) * LANES)
                xy_ref[2 * r, 8 * part + o : 8 * part + o + 1, :] = x[:, cut]
                xy_ref[2 * r + 1, 8 * part + o : 8 * part + o + 1, :] = y[:, cut]

    gather_near((1,))
    te_rows = te_of(1)
    te_out[...] = jnp.concatenate(
        [te_rows[:, n * LANES : (n + 1) * LANES] for n in range(4)] + [jnp.zeros((4, LANES), jnp.float32)], axis=0
    )
    upward = [
        pltpu.make_async_remote_copy(
            src_ref=src, dst_ref=dst, send_sem=carry_send.at[n], recv_sem=carry_recv.at[n],
            device_id=(above, member), device_id_type=mesh_id)
        for n, (src, dst) in enumerate(((near_ref.at[1], near_ref.at[3]), (te_out, te_in)))
    ]
    for copy in upward:
        copy.start()
    gather_near((0,))
    lower0, upper0 = cycle_loads(0, 1, te_of(0))
    send_on()
    gather_window((0, 1), (0, 1, 2))
    for copy in planes:
        copy.wait_recv()
    gather_window((0, 1), (3,))
    elements(0)
    for copy in upward:
        copy.wait_recv()
    te_below = jnp.concatenate([te_in[n : n + 1, :] for n in range(4)], axis=1)
    _, upper_below = cycle_loads(3, 0, te_below)
    for copy in forwards:
        copy.wait_recv()
    gather_near((2,))
    lower1, _ = cycle_loads(1, 2, te_rows)
    values = jnp.concatenate([lower0 + upper_below, lower1 + upper0], axis=0)
    high, rest = split(values)
    middle, low3 = split(rest)
    place = (iota((WIDE, WIDE), 0) == jnp.broadcast_to(rows_of[1], (WIDE, WIDE))).astype(jnp.float32)
    placed = nt(jnp.concatenate([high, middle, low3], axis=0), place)
    placed = placed[0:16] + placed[16:32] + placed[32:48]
    load_ref[:, 0, :] = placed[0:6]
    load_ref[:, 1, :] = placed[8:14]
    gather_window((2,), (0, 1, 2, 3))
    elements(1)

    width = thick_ref.shape[1]
    back = lax.rem(width - start, width)
    te_span = pltpu.roll(effective, back, 1)[:, :MOST]
    growth_span = pltpu.roll(growth, back, 1)[:, :MOST]
    offset = start - first * groups
    sub = iota((8, LANES), 0)
    for b in range(MOST // LANES):
        n = lane + (b * LANES + offset)
        o_of, k_of = n % groups, n // groups
        cut = slice(b * LANES, (b + 1) * LANES)
        keep = lane[0:1] + b * LANES < count
        for r in range(2):
            both = []
            for z in range(2):
                total = 0.0
                for e in range(groups // 8):
                    picked = lane_gather(xy_ref[2 * r + z, 8 * e : 8 * e + 8, :], k_of)
                    total = total + jnp.sum(jnp.where(o_of == sub + 8 * e, picked, 0.0), axis=0, keepdims=True)
                both.append(total)
            te = te_span[r : r + 1, cut]
            g = growth_span[r : r + 1, cut] * (both[0] + 3.0 * te * te * both[1])
            grad_ref[r : r + 1, cut] = jnp.where(keep, g, 0.0)

    for copy in rims + adjs + planes + forwards + upward:
        copy.wait_send()


def on_device(
    adjoint, mode_fields, node_slot, thickness, weld_land, panel_spans, load_factor,
    membrane, bending, geometric, stress_map,
):
    column_width = mode_fields.shape[3]
    groups = lax.axis_size("mer")
    rings = lax.axis_size("circ")
    tiles = column_width // LANES
    mode_rows = mode_fields.reshape(3, 6, 2, tiles, LANES).transpose(0, 1, 3, 2, 4).reshape(-1, LANES)
    adj_rows = adjoint.reshape(6, 2, 2, LANES).transpose(0, 2, 1, 3).reshape(-1, LANES)
    vmem = pl.BlockSpec(memory_space=pltpu.VMEM)
    hbm = pl.BlockSpec(memory_space=pltpu.HBM)
    half_groups = groups // 2
    dma = pltpu.SemaphoreType.DMA
    return pl.pallas_call(
        functools.partial(whole_kernel, groups, rings, tiles),
        out_shape=(
            jax.ShapeDtypeStruct((6, 2, WIDE), jnp.float32),
            jax.ShapeDtypeStruct((2, MOST), jnp.float32),
        ),
        in_specs=[hbm] * 11,
        out_specs=(vmem, vmem),
        scratch_shapes=[
            pltpu.VMEM((3, 4, 8, column_width), jnp.float32),
            pltpu.VMEM((groups, WIDE), jnp.int32),
            pltpu.VMEM((2, groups, WIDE), jnp.float32),
            pltpu.VMEM((3, 32, (groups + 1) * LANES), jnp.float32),
            pltpu.VMEM((4, 16, 3 * WIDE), jnp.float32),
            pltpu.VMEM((4, groups, LANES), jnp.float32),
            pltpu.VMEM((8, LANES), jnp.float32),
            pltpu.VMEM((8, LANES), jnp.float32),
            dma((groups,)), dma((groups,)),
            dma((half_groups,)), dma((half_groups,)),
            dma((half_groups,)), dma((half_groups,)),
            dma((half_groups,)), dma((half_groups,)),
            dma((2,)), dma((2,)),
            pltpu.VMEM((tiles, LANES), jnp.int32),
            pltpu.SMEM((1, groups), jnp.int32),
            pltpu.SMEM((1, 1), jnp.float32),
            pltpu.VMEM((2, column_width), jnp.float32),
            pltpu.VMEM((2, column_width), jnp.int32),
            pltpu.VMEM(mode_rows.shape, jnp.float32),
            pltpu.VMEM(adj_rows.shape, jnp.float32),
            pltpu.VMEM((24, 24), jnp.float32),
            pltpu.VMEM((24, 24), jnp.float32),
            pltpu.VMEM((3, 24, 24), jnp.float32),
            pltpu.VMEM((3, 24), jnp.float32),
            dma((11,)),
        ],
        compiler_params=pltpu.CompilerParams(
            vmem_limit_bytes=60 * 1024 * 1024, collective_id=0, has_side_effects=True
        ),
    )(
        node_slot.reshape(tiles, LANES), panel_spans, load_factor.reshape(1, 1), thickness, weld_land,
        mode_rows, adj_rows, membrane, bending, geometric, stress_map,
    )


def solution(mesh):
    return jax.shard_map(
        on_device,
        mesh=mesh,
        in_specs=(
            P(None, "circ", "mer"),
            P(None, None, "circ", None),
            P(),
            P("circ", None),
            P("circ", None),
            P("circ", None),
            P(),
            P(),
            P(),
            P(),
            P(),
        ),
        out_specs=(P(None, "circ", "mer"), P("circ", "mer")),
        check_vma=False,
    )
```

```python
import functools
import jax
import jax.numpy as jnp
from jax import lax
from jax.experimental import pallas as pl
from jax.experimental.pallas import tpu as pltpu
from jax.sharding import PartitionSpec as P

MOST = 768
LANES = 128
WIDE = 256


def lane_gather(x, index):
    return jnp.take_along_axis(x, index, axis=1, mode="promise_in_bounds")


def split(x):
    high = x.astype(jnp.bfloat16).astype(jnp.float32)
    return high, x - high


def gather_wide(block, low_index, in_low):
    left = lane_gather(block[:, :LANES], low_index)
    right = lane_gather(block[:, LANES:], low_index)
    return jnp.where(in_low, left, right)


def iota(shape, axis):
    return lax.broadcasted_iota(jnp.int32, shape, axis)


def untangle(turned, column, positions, groups, stride=1):
    width = LANES // groups
    tile = (positions // width) * stride + column
    within = positions % width
    parts = []
    for eight in range(groups // 8):
        total = None
        for q in range(width):
            base = groups * q + 8 * eight
            picked = lane_gather(turned[base : base + 8, :], tile)
            total = picked if total is None else jnp.where(within == q, picked, total)
        parts.append(total)
    return parts


def down(x):
    return jnp.sum(x, axis=0, keepdims=True)


def stack_corners(lower_here, upper_here, upper_next, lower_next):
    return jnp.concatenate([lower_here, upper_here, upper_next, lower_next], axis=0)


def triple(v):
    high, low = split(v)
    return jnp.concatenate([high, high, low], axis=0)


def nt(a, b):
    return lax.dot_general(a, b, (((1,), (1,)), ((), ())), preferred_element_type=jnp.float32)


def mm(a, b):
    return jnp.dot(a, b, preferred_element_type=jnp.float32)


def prepared_mats(membrane, bending, geometric, stress_map):
    stress = jnp.concatenate([stress_map, jnp.zeros((5, 24), jnp.float32)], axis=0)
    stacked = jnp.concatenate([membrane, bending, geometric[0], geometric[1], geometric[2], stress], axis=0)
    high, low = split(stacked)
    i, j = iota((24, 96), 0), iota((24, 96), 1)
    lands = (j % 8 < 6) & (i == 6 * (j % 32 // 8) + j % 8)
    from_low = j // 32 == 1
    put_high = jnp.where(lands & jnp.logical_not(from_low), 1.0, 0.0)
    put_low = jnp.where(lands & from_low, 1.0, 0.0)
    wide = mm(high, put_high) + mm(low, put_low)
    row, source = iota((168, 128), 0), iota((168, 128), 1)
    within = row % 32
    square = (row < 160) & (within % 8 < 6) & (source == 24 * (row // 32) + 6 * (within // 8) + within % 8)
    plain = (row >= 160) & (source == row - 40)
    mats = mm(jnp.where(square | plain, 1.0, 0.0), wide)
    k, c = iota((32, 24), 0), iota((32, 24), 1)
    pick = jnp.where((k % 8 < 6) & (c == 6 * (k // 8) + k % 8), 1.0, 0.0)
    s_high, rest = split(stress)
    s_mid, s_low = split(rest)
    return mats, nt(pick, s_high) + nt(pick, s_mid) + nt(pick, s_low)


def whole_kernel(
    groups, rings, tiles, slot_far, span_far, factor_far, thick_far, weld_far, mode_far, adj_far,
    membrane_far, bending_far, geometric_far, stress_far,
    packed_ref,
    nodes_ref, index_ref, teff_ref, window_ref, near_ref, xy_ref, te_out, te_in,
    plane_send, plane_recv, adj_send, adj_recv, rim_send, rim_recv, fwd_send, fwd_recv, carry_send, carry_recv,
    slot_ref, span_ref, factor_ref, thick_ref, weld_ref, mode_ref, adj_ref,
    membrane_ref, bending_ref, geometric_ref, stress_ref, input_sem,
):
    mesh_id = pl.DeviceIdType.MESH
    far = (mode_far, adj_far, slot_far, span_far, factor_far, thick_far, weld_far,
           membrane_far, bending_far, geometric_far, stress_far)
    close = (mode_ref, adj_ref, slot_ref, span_ref, factor_ref, thick_ref, weld_ref,
             membrane_ref, bending_ref, geometric_ref, stress_ref)
    inputs = [pltpu.make_async_copy(a, b, input_sem.at[n]) for n, (a, b) in enumerate(zip(far, close))]
    for copy in inputs:
        copy.start()
    half_groups = groups // 2
    ring, member = lax.axis_index("circ"), lax.axis_index("mer")
    below, above = lax.rem(ring + rings - 1, rings), lax.rem(ring + 1, rings)
    parity, pair_of = member % 2, member // 2
    same = [2 * lax.rem(pair_of + i, half_groups) + parity for i in range(half_groups)]

    barrier = pltpu.get_barrier_semaphore()
    for d in range(1, groups):
        pl.semaphore_signal(barrier, inc=1, device_id=(ring, lax.rem(member + d, groups)), device_id_type=mesh_id)
    for i in range(half_groups):
        pl.semaphore_signal(barrier, inc=1, device_id=(below, same[i]), device_id_type=mesh_id)
        pl.semaphore_signal(barrier, inc=1, device_id=(above, same[i]), device_id_type=mesh_id)

    for copy in inputs[:2]:
        copy.wait()
    empty = jnp.zeros((2, LANES), jnp.float32)
    own = pl.multiple_of(member * WIDE, WIDE)
    stride = 2 * tiles
    for f in range(2):
        near_ref[3, f, 6:8, :] = jnp.zeros((2, 3 * WIDE), jnp.float32)
    for f in range(4):
        nodes_ref[2, f, 6:8, :] = jnp.zeros((2, tiles * LANES), jnp.float32)
    for o in range(groups):
        for q in range(2):
            nodes_ref[q, 3, 6:8, o * WIDE : (o + 1) * WIDE] = jnp.zeros((2, WIDE), jnp.float32)
    for q in range(2):
        for f in range(3):
            for t in range(tiles):
                six = mode_ref[pl.ds(f * 6 * stride + 2 * t + q, 6, stride=stride), :]
                nodes_ref[q, f, :, t * LANES : (t + 1) * LANES] = jnp.concatenate([six, empty], axis=0)
        for t in range(2):
            six = adj_ref[pl.ds(2 * t + q, 6, stride=4), :]
            nodes_ref[q, 3, 0:6, pl.ds(own + t * LANES, LANES)] = six
    pl.semaphore_wait(barrier, groups - 1 + 2 * half_groups)

    def block_of(owner):
        return pl.ds(pl.multiple_of(owner * WIDE, WIDE), WIDE)

    rims, adjs, planes, forwards = [], [], [], []
    owners_same = [2 * lax.rem(pair_of + half_groups - i, half_groups) + parity for i in range(half_groups)]
    for i in range(half_groups):
        adjs.append(pltpu.make_async_remote_copy(
            src_ref=nodes_ref.at[0, pl.ds(3, 1), pl.ds(0, 6), block_of(member)],
            dst_ref=nodes_ref.at[2, pl.ds(3, 1), pl.ds(0, 6), block_of(member)],
            send_sem=adj_send.at[i], recv_sem=adj_recv.at[i],
            device_id=(below, same[i]), device_id_type=mesh_id))
        rims.append(pltpu.make_async_remote_copy(
            src_ref=nodes_ref.at[0, pl.ds(0, 3), pl.ds(0, 6), block_of(owners_same[i])],
            dst_ref=nodes_ref.at[2, pl.ds(0, 3), pl.ds(0, 6), block_of(owners_same[i])],
            send_sem=rim_send.at[i], recv_sem=rim_recv.at[i],
            device_id=(below, member), device_id_type=mesh_id))
        adjs[i].start()
        rims[i].start()
    for d in range(1, groups):
        planes.append(pltpu.make_async_remote_copy(
            src_ref=nodes_ref.at[pl.ds(0, 2), pl.ds(3, 1), pl.ds(0, 6), block_of(member)],
            dst_ref=nodes_ref.at[pl.ds(0, 2), pl.ds(3, 1), pl.ds(0, 6), block_of(member)],
            send_sem=plane_send.at[d], recv_sem=plane_recv.at[d],
            device_id=(ring, lax.rem(member + d, groups)), device_id_type=mesh_id))
        planes[-1].start()
    for i in range(half_groups):
        forwards.append(pltpu.make_async_remote_copy(
            src_ref=nodes_ref.at[2, pl.ds(0, 4), pl.ds(0, 6), block_of(owners_same[i])],
            dst_ref=nodes_ref.at[2, pl.ds(0, 4), pl.ds(0, 6), block_of(owners_same[i])],
            send_sem=fwd_send.at[i], recv_sem=fwd_recv.at[i],
            device_id=(ring, member + 1 - 2 * parity), device_id_type=mesh_id))

    def send_on():
        for i in range(half_groups):
            adjs[i].wait_recv()
            rims[i].wait_recv()
            forwards[i].start()

    for copy in inputs[2:]:
        copy.wait()
    factor = factor_ref[0, 0]
    start = jnp.int32(0)
    count = jnp.int32(0)
    for g in range(groups):
        start = start + jnp.where(g < member, span_ref[0, g], 0)
        count = count + jnp.where(g == member, span_ref[0, g], 0)
    first = start // groups
    lane = iota((8, LANES), 1)

    pad = jnp.zeros((LANES - tiles, LANES), jnp.int32)
    slots = jnp.concatenate([slot_ref[...], pad], axis=0) % WIDE
    slots_t = slots.astype(jnp.float32).T.astype(jnp.int32)
    for half in range(2):
        for e, part in enumerate(untangle(slots_t, 0, lane + half * LANES, groups)):
            index_ref[8 * e : 8 * e + 8, half * LANES : (half + 1) * LANES] = part
    shifted = untangle(slots_t, 0, (first + lane) % WIDE, groups)

    growth = 1.0 + 0.5 * weld_ref[...].astype(jnp.float32)
    effective = thick_ref[...] * growth
    for cycle in range(2):
        rows = [effective[cycle : cycle + 1, t * LANES : (t + 1) * LANES] for t in range(tiles)]
        natural = jnp.concatenate(rows + [jnp.zeros((LANES - tiles, LANES), jnp.float32)], axis=0)
        natural_t = natural.T
        for half in range(2):
            for e, part in enumerate(untangle(natural_t, 0, lane + half * LANES, groups)):
                teff_ref[cycle, 8 * e : 8 * e + 8, half * LANES : (half + 1) * LANES] = part

    mats, map_t = prepared_mats(membrane_ref[...], bending_ref[...], geometric_ref[...], stress_ref[...])

    owners, rows_of = [], []
    for d in (-1, 0, 1):
        owner = lax.rem(member + d + groups, groups)
        row = index_ref[pl.ds(owner, 1), :]
        if d == -1:
            row = jnp.where(member == 0, pltpu.roll(row, 1, 1), row)
        if d == 1:
            row = jnp.where(member == groups - 1, pltpu.roll(row, WIDE - 1, 1), row)
        owners.append(owner)
        rows_of.append(row)
    def gather_near(cycles):
        for d in range(3):
            base = pl.multiple_of(owners[d] * WIDE, WIDE)
            wide = jnp.broadcast_to(rows_of[d], (8, WIDE))
            for half in range(2):
                index = wide[:, half * LANES : (half + 1) * LANES]
                low, in_low = index % LANES, index < LANES
                for q in cycles:
                    for f in range(2):
                        block = nodes_ref[q, f, :, pl.ds(base, WIDE)]
                        near_ref[q, f, :, d * WIDE + half * LANES : d * WIDE + (half + 1) * LANES] = (
                            gather_wide(block, low, in_low)
                        )

    behind = lax.rem(member + groups - 1, groups)

    def te_of(r):
        te_behind = teff_ref[r, pl.ds(behind, 1), :]
        te_behind = jnp.where(member == 0, pltpu.roll(te_behind, 1, 1), te_behind)
        return jnp.concatenate([te_behind, teff_ref[r, pl.ds(member, 1), :]], axis=1)

    def cycle_loads(lower, upper, te):
        pair = [0.0, 0.0, 0.0]
        for f in range(2):
            v = stack_corners(
                near_ref[lower, f, :, : 2 * WIDE],
                near_ref[upper, f, :, : 2 * WIDE],
                near_ref[upper, f, :, WIDE:],
                near_ref[lower, f, :, WIDE:],
            )
            product = mm(mats[64:160], triple(v))
            for s in range(3):
                pair[s] = pair[s] + down(v * product[32 * s : 32 * s + 32])
        spread = 0.0
        for s in range(3):
            spread = spread + map_t[:, s : s + 1] * pair[s]
        spread = spread * (factor * te)
        return (
            spread[0:8, WIDE:] + spread[24:32, :WIDE],
            spread[8:16, WIDE:] + spread[16:24, :WIDE],
        )

    def gather_window(cycles, fields):
        for o in range(groups):
            index = jnp.broadcast_to(shifted[o // 8][o % 8 : o % 8 + 1, :], (8, LANES))
            low, in_low = index % LANES, index < LANES
            for q in cycles:
                for f in fields:
                    block = nodes_ref[q, f, :, o * WIDE : (o + 1) * WIDE]
                    got = gather_wide(block, low, in_low)
                    window_ref[q, 8 * f : 8 * f + 8, o * LANES : (o + 1) * LANES] = got
                    if o == 0:
                        window_ref[q, 8 * f : 8 * f + 8, groups * LANES : (groups + 1) * LANES] = pltpu.roll(
                            got, LANES - 1, 1
                        )

    size = 8 * LANES
    def elements(r):
        for part in range(groups // 8):
            here = slice(part * size, (part + 1) * size)
            after = slice(part * size + LANES, (part + 1) * size + LANES)

            def corner(f):
                rows = slice(8 * f, 8 * f + 8)
                return stack_corners(
                    window_ref[r, rows, here],
                    window_ref[r + 1, rows, here],
                    window_ref[r + 1, rows, after],
                    window_ref[r, rows, after],
                )

            quad = [0.0] * 5
            for f in range(2):
                v = corner(f)
                product = mm(mats, triple(v))[:160]
                for s in range(5):
                    quad[s] = quad[s] + v * product[32 * s : 32 * s + 32]
            u, a = corner(2), corner(3)
            u_three = triple(u)
            tangent = mm(mats[0:64], u_three)
            stress = mm(mats[160:168], u_three)
            geometric = 0.0
            for s in range(3):
                geometric = geometric + stress[s : s + 1] * down(quad[2 + s])
            x = down(quad[0] - a * tangent[0:32]) - factor * geometric
            y = down(quad[1] - a * tangent[32:64])
            for o in range(8):
                cut = slice(o * LANES, (o + 1) * LANES)
                xy_ref[2 * r, 8 * part + o : 8 * part + o + 1, :] = x[:, cut]
                xy_ref[2 * r + 1, 8 * part + o : 8 * part + o + 1, :] = y[:, cut]

    gather_near((1,))
    te_rows = te_of(1)
    te_out[...] = jnp.concatenate(
        [te_rows[:, n * LANES : (n + 1) * LANES] for n in range(4)] + [jnp.zeros((4, LANES), jnp.float32)], axis=0
    )
    upward = [
        pltpu.make_async_remote_copy(
            src_ref=src, dst_ref=dst, send_sem=carry_send.at[n], recv_sem=carry_recv.at[n],
            device_id=(above, member), device_id_type=mesh_id)
        for n, (src, dst) in enumerate((
            (near_ref.at[1, pl.ds(0, 2), pl.ds(0, 6)], near_ref.at[3, pl.ds(0, 2), pl.ds(0, 6)]), (te_out, te_in),
        ))
    ]
    for copy in upward:
        copy.start()
    gather_near((0,))
    lower0, upper0 = cycle_loads(0, 1, te_of(0))
    send_on()
    gather_window((0, 1), (0, 1, 2))
    for copy in planes:
        copy.wait_recv()
    gather_window((0, 1), (3,))
    elements(0)
    for copy in upward:
        copy.wait_recv()
    te_below = jnp.concatenate([te_in[n : n + 1, :] for n in range(4)], axis=1)
    _, upper_below = cycle_loads(3, 0, te_below)
    for copy in forwards:
        copy.wait_recv()
    gather_near((2,))
    lower1, _ = cycle_loads(1, 2, te_rows)
    values = jnp.concatenate([lower0 + upper_below, lower1 + upper0], axis=0)
    high, rest = split(values)
    middle, low3 = split(rest)
    place = (iota((WIDE, WIDE), 0) == jnp.broadcast_to(rows_of[1], (WIDE, WIDE))).astype(jnp.float32)
    placed = nt(jnp.concatenate([high, middle, low3], axis=0), place)
    placed = placed[0:16] + placed[16:32] + placed[32:48]
    for q in range(2):
        for h in range(2):
            at = 16 * q + 8 * h
            packed_ref[at : at + 8, :] = placed[8 * q : 8 * q + 8, h * LANES : (h + 1) * LANES]
    gather_window((2,), (0, 1, 2, 3))
    elements(1)

    width = thick_ref.shape[1]
    back = lax.rem(width - start, width)
    te_span = pltpu.roll(effective, back, 1)[:, :MOST]
    growth_span = pltpu.roll(growth, back, 1)[:, :MOST]
    offset = start - first * groups
    sub = iota((8, LANES), 0)
    for b in range(MOST // LANES):
        n = lane + (b * LANES + offset)
        o_of, k_of = n % groups, n // groups
        cut = slice(b * LANES, (b + 1) * LANES)
        keep = lane[0:1] + b * LANES < count
        for r in range(2):
            both = []
            for z in range(2):
                total = 0.0
                for e in range(groups // 8):
                    picked = lane_gather(xy_ref[2 * r + z, 8 * e : 8 * e + 8, :], k_of)
                    total = total + jnp.sum(jnp.where(o_of == sub + 8 * e, picked, 0.0), axis=0, keepdims=True)
                both.append(total)
            te = te_span[r : r + 1, cut]
            g = growth_span[r : r + 1, cut] * (both[0] + 3.0 * te * te * both[1])
            at = 32 + r * (MOST // LANES) + b
            packed_ref[at : at + 1, :] = jnp.where(keep, g, 0.0)

    for copy in rims + adjs + planes + forwards + upward:
        copy.wait_send()


def unpack_kernel(packed_ref, load_ref, grad_ref):
    blocks = MOST // LANES
    for q in range(2):
        for h in range(2):
            at = 16 * q + 8 * h
            load_ref[:, q, h * LANES : (h + 1) * LANES] = packed_ref[at : at + 6, :]
    for r in range(2):
        for b in range(blocks):
            at = 32 + r * blocks + b
            grad_ref[r : r + 1, b * LANES : (b + 1) * LANES] = packed_ref[at : at + 1, :]


def on_device(
    adjoint, mode_fields, node_slot, thickness, weld_land, panel_spans, load_factor,
    membrane, bending, geometric, stress_map,
):
    column_width = mode_fields.shape[3]
    groups = lax.axis_size("mer")
    rings = lax.axis_size("circ")
    tiles = column_width // LANES
    mode_rows = mode_fields.reshape(3, 6, 2, tiles, LANES).transpose(0, 1, 3, 2, 4).reshape(-1, LANES)
    adj_rows = adjoint.reshape(6, 2, 2, LANES).transpose(0, 2, 1, 3).reshape(-1, LANES)
    vmem = pl.BlockSpec(memory_space=pltpu.VMEM)
    hbm = pl.BlockSpec(memory_space=pltpu.HBM)
    half_groups = groups // 2
    dma = pltpu.SemaphoreType.DMA
    packed = pl.pallas_call(
        functools.partial(whole_kernel, groups, rings, tiles),
        out_shape=jax.ShapeDtypeStruct((32 + 2 * MOST // LANES, LANES), jnp.float32),
        in_specs=[hbm] * 11,
        out_specs=vmem,
        scratch_shapes=[
            pltpu.VMEM((3, 4, 8, column_width), jnp.float32),
            pltpu.VMEM((groups, WIDE), jnp.int32),
            pltpu.VMEM((2, groups, WIDE), jnp.float32),
            pltpu.VMEM((3, 32, (groups + 1) * LANES), jnp.float32),
            pltpu.VMEM((4, 2, 8, 3 * WIDE), jnp.float32),
            pltpu.VMEM((4, groups, LANES), jnp.float32),
            pltpu.VMEM((8, LANES), jnp.float32),
            pltpu.VMEM((8, LANES), jnp.float32),
            dma((groups,)), dma((groups,)),
            dma((half_groups,)), dma((half_groups,)),
            dma((half_groups,)), dma((half_groups,)),
            dma((half_groups,)), dma((half_groups,)),
            dma((2,)), dma((2,)),
            pltpu.VMEM((tiles, LANES), jnp.int32),
            pltpu.SMEM((1, groups), jnp.int32),
            pltpu.SMEM((1, 1), jnp.float32),
            pltpu.VMEM((2, column_width), jnp.float32),
            pltpu.VMEM((2, column_width), jnp.int32),
            pltpu.VMEM(mode_rows.shape, jnp.float32),
            pltpu.VMEM(adj_rows.shape, jnp.float32),
            pltpu.VMEM((24, 24), jnp.float32),
            pltpu.VMEM((24, 24), jnp.float32),
            pltpu.VMEM((3, 24, 24), jnp.float32),
            pltpu.VMEM((3, 24), jnp.float32),
            dma((11,)),
        ],
        compiler_params=pltpu.CompilerParams(
            vmem_limit_bytes=60 * 1024 * 1024, collective_id=0, has_side_effects=True
        ),
    )(
        node_slot.reshape(tiles, LANES), panel_spans, load_factor.reshape(1, 1), thickness, weld_land,
        mode_rows, adj_rows, membrane, bending, geometric, stress_map,
    )
    return pl.pallas_call(
        unpack_kernel,
        out_shape=(
            jax.ShapeDtypeStruct((6, 2, WIDE), jnp.float32),
            jax.ShapeDtypeStruct((2, MOST), jnp.float32),
        ),
        in_specs=[vmem],
        out_specs=(vmem, vmem),
    )(packed)


def solution(mesh):
    return jax.shard_map(
        on_device,
        mesh=mesh,
        in_specs=(
            P(None, "circ", "mer"),
            P(None, None, "circ", None),
            P(),
            P("circ", None),
            P("circ", None),
            P("circ", None),
            P(),
            P(),
            P(),
            P(),
            P(),
        ),
        out_specs=(P(None, "circ", "mer"), P("circ", "mer")),
        check_vma=False,
    )
```

```python
import functools
import jax
import jax.numpy as jnp
from jax import lax
from jax.experimental import pallas as pl
from jax.experimental.pallas import tpu as pltpu
from jax.sharding import PartitionSpec as P

MOST = 768
LANES = 128
WIDE = 256


def lane_gather(x, index):
    return jnp.take_along_axis(x, index, axis=1, mode="promise_in_bounds")


def split(x):
    high = x.astype(jnp.bfloat16).astype(jnp.float32)
    return high, x - high


def gather_wide(block, low_index, in_low):
    left = lane_gather(block[:, :LANES], low_index)
    right = lane_gather(block[:, LANES:], low_index)
    return jnp.where(in_low, left, right)


def iota(shape, axis):
    return lax.broadcasted_iota(jnp.int32, shape, axis)


def untangle(turned, column, positions, groups, stride=1):
    width = LANES // groups
    tile = (positions // width) * stride + column
    within = positions % width
    parts = []
    for eight in range(groups // 8):
        total = None
        for q in range(width):
            base = groups * q + 8 * eight
            picked = lane_gather(turned[base : base + 8, :], tile)
            total = picked if total is None else jnp.where(within == q, picked, total)
        parts.append(total)
    return parts


def down(x):
    return jnp.sum(x, axis=0, keepdims=True)


def stack_corners(lower_here, upper_here, upper_next, lower_next):
    return jnp.concatenate([lower_here, upper_here, upper_next, lower_next], axis=0)


def triple(v):
    high, low = split(v)
    return jnp.concatenate([high, high, low], axis=0)


def nt(a, b):
    return lax.dot_general(a, b, (((1,), (1,)), ((), ())), preferred_element_type=jnp.float32)


def mm(a, b):
    return jnp.dot(a, b, preferred_element_type=jnp.float32)


def prepared_mats(membrane, bending, geometric, stress_map):
    stress = jnp.concatenate([stress_map, jnp.zeros((5, 24), jnp.float32)], axis=0)
    stacked = jnp.concatenate([membrane, bending, geometric[0], geometric[1], geometric[2], stress], axis=0)
    high, low = split(stacked)
    i, j = iota((24, 96), 0), iota((24, 96), 1)
    lands = (j % 8 < 6) & (i == 6 * (j % 32 // 8) + j % 8)
    from_low = j // 32 == 1
    put_high = jnp.where(lands & jnp.logical_not(from_low), 1.0, 0.0)
    put_low = jnp.where(lands & from_low, 1.0, 0.0)
    wide = mm(high, put_high) + mm(low, put_low)
    row, source = iota((168, 128), 0), iota((168, 128), 1)
    within = row % 32
    square = (row < 160) & (within % 8 < 6) & (source == 24 * (row // 32) + 6 * (within // 8) + within % 8)
    plain = (row >= 160) & (source == row - 40)
    mats = mm(jnp.where(square | plain, 1.0, 0.0), wide)
    k, c = iota((32, 24), 0), iota((32, 24), 1)
    pick = jnp.where((k % 8 < 6) & (c == 6 * (k // 8) + k % 8), 1.0, 0.0)
    s_high, rest = split(stress)
    s_mid, s_low = split(rest)
    return mats, nt(pick, s_high) + nt(pick, s_mid) + nt(pick, s_low)


def whole_kernel(
    groups, rings, tiles, slot_far, span_far, factor_far, thick_far, weld_far, mode_far, adj_far,
    membrane_far, bending_far, geometric_far, stress_far,
    packed_ref,
    nodes_ref, index_ref, teff_ref, window_ref, near_ref, xy_ref, te_out, te_in,
    plane_send, plane_recv, adj_send, adj_recv, rim_send, rim_recv, fwd_send, fwd_recv, carry_send, carry_recv,
    slot_ref, span_ref, factor_ref, thick_ref, weld_ref, mode_ref, adj_ref,
    membrane_ref, bending_ref, geometric_ref, stress_ref, input_sem,
):
    mesh_id = pl.DeviceIdType.MESH
    far = (mode_far, adj_far, slot_far, span_far, factor_far, thick_far, weld_far,
           membrane_far, bending_far, geometric_far, stress_far)
    close = (mode_ref, adj_ref, slot_ref, span_ref, factor_ref, thick_ref, weld_ref,
             membrane_ref, bending_ref, geometric_ref, stress_ref)
    inputs = [pltpu.make_async_copy(a, b, input_sem.at[n]) for n, (a, b) in enumerate(zip(far, close))]
    for copy in inputs:
        copy.start()
    half_groups = groups // 2
    ring, member = lax.axis_index("circ"), lax.axis_index("mer")
    below, above = lax.rem(ring + rings - 1, rings), lax.rem(ring + 1, rings)
    parity, pair_of = member % 2, member // 2
    same = [2 * lax.rem(pair_of + i, half_groups) + parity for i in range(half_groups)]

    barrier = pltpu.get_barrier_semaphore()
    for d in range(1, groups):
        pl.semaphore_signal(barrier, inc=1, device_id=(ring, lax.rem(member + d, groups)), device_id_type=mesh_id)
    for i in range(half_groups):
        pl.semaphore_signal(barrier, inc=1, device_id=(below, same[i]), device_id_type=mesh_id)
        pl.semaphore_signal(barrier, inc=1, device_id=(above, same[i]), device_id_type=mesh_id)

    for copy in inputs[:2]:
        copy.wait()
    empty = jnp.zeros((2, LANES), jnp.float32)
    own = pl.multiple_of(member * WIDE, WIDE)
    stride = 2 * tiles
    for f in range(2):
        near_ref[3, f, 6:8, :] = jnp.zeros((2, 3 * WIDE), jnp.float32)
    for f in range(4):
        nodes_ref[2, f, 6:8, :] = jnp.zeros((2, tiles * LANES), jnp.float32)
    for o in range(groups):
        for q in range(2):
            nodes_ref[q, 3, 6:8, o * WIDE : (o + 1) * WIDE] = jnp.zeros((2, WIDE), jnp.float32)
    for q in range(2):
        for f in range(3):
            for t in range(tiles):
                six = mode_ref[pl.ds(f * 6 * stride + 2 * t + q, 6, stride=stride), :]
                nodes_ref[q, f, :, t * LANES : (t + 1) * LANES] = jnp.concatenate([six, empty], axis=0)
        for t in range(2):
            six = adj_ref[pl.ds(2 * t + q, 6, stride=4), :]
            nodes_ref[q, 3, 0:6, pl.ds(own + t * LANES, LANES)] = six
    pl.semaphore_wait(barrier, groups - 1 + 2 * half_groups)

    def block_of(owner):
        return pl.ds(pl.multiple_of(owner * WIDE, WIDE), WIDE)

    rims, adjs, planes, forwards = [], [], [], []
    owners_same = [2 * lax.rem(pair_of + half_groups - i, half_groups) + parity for i in range(half_groups)]
    for i in range(half_groups):
        adjs.append(pltpu.make_async_remote_copy(
            src_ref=nodes_ref.at[0, pl.ds(3, 1), pl.ds(0, 6), block_of(member)],
            dst_ref=nodes_ref.at[2, pl.ds(3, 1), pl.ds(0, 6), block_of(member)],
            send_sem=adj_send.at[i], recv_sem=adj_recv.at[i],
            device_id=(below, same[i]), device_id_type=mesh_id))
        rims.append(pltpu.make_async_remote_copy(
            src_ref=nodes_ref.at[0, pl.ds(0, 3), pl.ds(0, 6), block_of(owners_same[i])],
            dst_ref=nodes_ref.at[2, pl.ds(0, 3), pl.ds(0, 6), block_of(owners_same[i])],
            send_sem=rim_send.at[i], recv_sem=rim_recv.at[i],
            device_id=(below, member), device_id_type=mesh_id))
        rims[i].start()
        adjs[i].start()
    for d in range(1, groups):
        planes.append(pltpu.make_async_remote_copy(
            src_ref=nodes_ref.at[pl.ds(0, 2), pl.ds(3, 1), pl.ds(0, 6), block_of(member)],
            dst_ref=nodes_ref.at[pl.ds(0, 2), pl.ds(3, 1), pl.ds(0, 6), block_of(member)],
            send_sem=plane_send.at[d], recv_sem=plane_recv.at[d],
            device_id=(ring, lax.rem(member + d, groups)), device_id_type=mesh_id))
        planes[-1].start()
    for i in range(half_groups):
        forwards.append(pltpu.make_async_remote_copy(
            src_ref=nodes_ref.at[2, pl.ds(0, 4), pl.ds(0, 6), block_of(owners_same[i])],
            dst_ref=nodes_ref.at[2, pl.ds(0, 4), pl.ds(0, 6), block_of(owners_same[i])],
            send_sem=fwd_send.at[i], recv_sem=fwd_recv.at[i],
            device_id=(ring, member + 1 - 2 * parity), device_id_type=mesh_id))

    def send_on():
        for i in range(half_groups):
            adjs[i].wait_recv()
            rims[i].wait_recv()
            forwards[i].start()

    for copy in inputs[2:]:
        copy.wait()
    factor = factor_ref[0, 0]
    start = jnp.int32(0)
    count = jnp.int32(0)
    for g in range(groups):
        start = start + jnp.where(g < member, span_ref[0, g], 0)
        count = count + jnp.where(g == member, span_ref[0, g], 0)
    first = start // groups
    lane = iota((8, LANES), 1)

    pad = jnp.zeros((LANES - tiles, LANES), jnp.int32)
    slots = jnp.concatenate([slot_ref[...], pad], axis=0) % WIDE
    slots_t = slots.astype(jnp.float32).T.astype(jnp.int32)
    for half in range(2):
        for e, part in enumerate(untangle(slots_t, 0, lane + half * LANES, groups)):
            index_ref[8 * e : 8 * e + 8, half * LANES : (half + 1) * LANES] = part
    shifted = untangle(slots_t, 0, (first + lane) % WIDE, groups)

    growth = 1.0 + 0.5 * weld_ref[...].astype(jnp.float32)
    effective = thick_ref[...] * growth
    for cycle in range(2):
        rows = [effective[cycle : cycle + 1, t * LANES : (t + 1) * LANES] for t in range(tiles)]
        natural = jnp.concatenate(rows + [jnp.zeros((LANES - tiles, LANES), jnp.float32)], axis=0)
        natural_t = natural.T
        for half in range(2):
            for e, part in enumerate(untangle(natural_t, 0, lane + half * LANES, groups)):
                teff_ref[cycle, 8 * e : 8 * e + 8, half * LANES : (half + 1) * LANES] = part

    mats, map_t = prepared_mats(membrane_ref[...], bending_ref[...], geometric_ref[...], stress_ref[...])

    owners, rows_of = [], []
    for d in (-1, 0, 1):
        owner = lax.rem(member + d + groups, groups)
        row = index_ref[pl.ds(owner, 1), :]
        if d == -1:
            row = jnp.where(member == 0, pltpu.roll(row, 1, 1), row)
        if d == 1:
            row = jnp.where(member == groups - 1, pltpu.roll(row, WIDE - 1, 1), row)
        owners.append(owner)
        rows_of.append(row)
    def gather_near(cycles):
        for d in range(3):
            base = pl.multiple_of(owners[d] * WIDE, WIDE)
            wide = jnp.broadcast_to(rows_of[d], (8, WIDE))
            for half in range(2):
                index = wide[:, half * LANES : (half + 1) * LANES]
                low, in_low = index % LANES, index < LANES
                for q in cycles:
                    for f in range(2):
                        block = nodes_ref[q, f, :, pl.ds(base, WIDE)]
                        near_ref[q, f, :, d * WIDE + half * LANES : d * WIDE + (half + 1) * LANES] = (
                            gather_wide(block, low, in_low)
                        )

    behind = lax.rem(member + groups - 1, groups)

    def te_of(r):
        te_behind = teff_ref[r, pl.ds(behind, 1), :]
        te_behind = jnp.where(member == 0, pltpu.roll(te_behind, 1, 1), te_behind)
        return jnp.concatenate([te_behind, teff_ref[r, pl.ds(member, 1), :]], axis=1)

    def cycle_loads(lower, upper, te):
        pair = [0.0, 0.0, 0.0]
        for f in range(2):
            v = stack_corners(
                near_ref[lower, f, :, : 2 * WIDE],
                near_ref[upper, f, :, : 2 * WIDE],
                near_ref[upper, f, :, WIDE:],
                near_ref[lower, f, :, WIDE:],
            )
            product = mm(mats[64:160], triple(v))
            for s in range(3):
                pair[s] = pair[s] + down(v * product[32 * s : 32 * s + 32])
        spread = 0.0
        for s in range(3):
            spread = spread + map_t[:, s : s + 1] * pair[s]
        spread = spread * (factor * te)
        return (
            spread[0:8, WIDE:] + spread[24:32, :WIDE],
            spread[8:16, WIDE:] + spread[16:24, :WIDE],
        )

    def gather_window(cycles, fields):
        for o in range(groups):
            index = jnp.broadcast_to(shifted[o // 8][o % 8 : o % 8 + 1, :], (8, LANES))
            low, in_low = index % LANES, index < LANES
            for q in cycles:
                for f in fields:
                    block = nodes_ref[q, f, :, o * WIDE : (o + 1) * WIDE]
                    got = gather_wide(block, low, in_low)
                    window_ref[q, 8 * f : 8 * f + 8, o * LANES : (o + 1) * LANES] = got
                    if o == 0:
                        window_ref[q, 8 * f : 8 * f + 8, groups * LANES : (groups + 1) * LANES] = pltpu.roll(
                            got, LANES - 1, 1
                        )

    size = 8 * LANES
    def elements(r):
        for part in range(groups // 8):
            here = slice(part * size, (part + 1) * size)
            after = slice(part * size + LANES, (part + 1) * size + LANES)

            def corner(f):
                rows = slice(8 * f, 8 * f + 8)
                return stack_corners(
                    window_ref[r, rows, here],
                    window_ref[r + 1, rows, here],
                    window_ref[r + 1, rows, after],
                    window_ref[r, rows, after],
                )

            quad = [0.0] * 5
            for f in range(2):
                v = corner(f)
                product = mm(mats, triple(v))[:160]
                for s in range(5):
                    quad[s] = quad[s] + v * product[32 * s : 32 * s + 32]
            u, a = corner(2), corner(3)
            u_three = triple(u)
            tangent = mm(mats[0:64], u_three)
            stress = mm(mats[160:168], u_three)
            geometric = 0.0
            for s in range(3):
                geometric = geometric + stress[s : s + 1] * down(quad[2 + s])
            x = down(quad[0] - a * tangent[0:32]) - factor * geometric
            y = down(quad[1] - a * tangent[32:64])
            for o in range(8):
                cut = slice(o * LANES, (o + 1) * LANES)
                xy_ref[2 * r, 8 * part + o : 8 * part + o + 1, :] = x[:, cut]
                xy_ref[2 * r + 1, 8 * part + o : 8 * part + o + 1, :] = y[:, cut]

    gather_near((1,))
    te_rows = te_of(1)
    te_out[...] = jnp.concatenate(
        [te_rows[:, n * LANES : (n + 1) * LANES] for n in range(4)] + [jnp.zeros((4, LANES), jnp.float32)], axis=0
    )
    upward = [
        pltpu.make_async_remote_copy(
            src_ref=src, dst_ref=dst, send_sem=carry_send.at[n], recv_sem=carry_recv.at[n],
            device_id=(above, member), device_id_type=mesh_id)
        for n, (src, dst) in enumerate((
            (near_ref.at[1, pl.ds(0, 2), pl.ds(0, 6)], near_ref.at[3, pl.ds(0, 2), pl.ds(0, 6)]), (te_out, te_in),
        ))
    ]
    for copy in upward:
        copy.start()
    gather_near((0,))
    lower0, upper0 = cycle_loads(0, 1, te_of(0))
    gather_window((0, 1), (0, 1, 2))
    send_on()
    for copy in planes:
        copy.wait_recv()
    gather_window((0, 1), (3,))
    elements(0)
    for copy in upward:
        copy.wait_recv()
    te_below = jnp.concatenate([te_in[n : n + 1, :] for n in range(4)], axis=1)
    _, upper_below = cycle_loads(3, 0, te_below)
    for copy in forwards:
        copy.wait_recv()
    gather_near((2,))
    lower1, _ = cycle_loads(1, 2, te_rows)
    values = jnp.concatenate([lower0 + upper_below, lower1 + upper0], axis=0)
    high, rest = split(values)
    middle, low3 = split(rest)
    place = (iota((WIDE, WIDE), 0) == jnp.broadcast_to(rows_of[1], (WIDE, WIDE))).astype(jnp.float32)
    placed = nt(jnp.concatenate([high, middle, low3], axis=0), place)
    placed = placed[0:16] + placed[16:32] + placed[32:48]
    for q in range(2):
        for h in range(2):
            at = 16 * q + 8 * h
            packed_ref[at : at + 8, :] = placed[8 * q : 8 * q + 8, h * LANES : (h + 1) * LANES]
    gather_window((2,), (0, 1, 2, 3))
    elements(1)

    width = thick_ref.shape[1]
    back = lax.rem(width - start, width)
    te_span = pltpu.roll(effective, back, 1)[:, :MOST]
    growth_span = pltpu.roll(growth, back, 1)[:, :MOST]
    offset = start - first * groups
    sub = iota((8, LANES), 0)
    for b in range(MOST // LANES):
        n = lane + (b * LANES + offset)
        o_of, k_of = n % groups, n // groups
        cut = slice(b * LANES, (b + 1) * LANES)
        keep = lane[0:1] + b * LANES < count
        for r in range(2):
            both = []
            for z in range(2):
                total = 0.0
                for e in range(groups // 8):
                    picked = lane_gather(xy_ref[2 * r + z, 8 * e : 8 * e + 8, :], k_of)
                    total = total + jnp.sum(jnp.where(o_of == sub + 8 * e, picked, 0.0), axis=0, keepdims=True)
                both.append(total)
            te = te_span[r : r + 1, cut]
            g = growth_span[r : r + 1, cut] * (both[0] + 3.0 * te * te * both[1])
            at = 32 + r * (MOST // LANES) + b
            packed_ref[at : at + 1, :] = jnp.where(keep, g, 0.0)

    for copy in rims + adjs + planes + forwards + upward:
        copy.wait_send()


def unpack_kernel(packed_ref, load_ref, grad_ref):
    blocks = MOST // LANES
    for q in range(2):
        for h in range(2):
            at = 16 * q + 8 * h
            load_ref[:, q, h * LANES : (h + 1) * LANES] = packed_ref[at : at + 6, :]
    for r in range(2):
        for b in range(blocks):
            at = 32 + r * blocks + b
            grad_ref[r : r + 1, b * LANES : (b + 1) * LANES] = packed_ref[at : at + 1, :]


def on_device(
    adjoint, mode_fields, node_slot, thickness, weld_land, panel_spans, load_factor,
    membrane, bending, geometric, stress_map,
):
    column_width = mode_fields.shape[3]
    groups = lax.axis_size("mer")
    rings = lax.axis_size("circ")
    tiles = column_width // LANES
    mode_rows = mode_fields.reshape(3, 6, 2, tiles, LANES).transpose(0, 1, 3, 2, 4).reshape(-1, LANES)
    adj_rows = adjoint.reshape(6, 2, 2, LANES).transpose(0, 2, 1, 3).reshape(-1, LANES)
    vmem = pl.BlockSpec(memory_space=pltpu.VMEM)
    hbm = pl.BlockSpec(memory_space=pltpu.HBM)
    half_groups = groups // 2
    dma = pltpu.SemaphoreType.DMA
    packed = pl.pallas_call(
        functools.partial(whole_kernel, groups, rings, tiles),
        out_shape=jax.ShapeDtypeStruct((32 + 2 * MOST // LANES, LANES), jnp.float32),
        in_specs=[hbm] * 11,
        out_specs=vmem,
        scratch_shapes=[
            pltpu.VMEM((3, 4, 8, column_width), jnp.float32),
            pltpu.VMEM((groups, WIDE), jnp.int32),
            pltpu.VMEM((2, groups, WIDE), jnp.float32),
            pltpu.VMEM((3, 32, (groups + 1) * LANES), jnp.float32),
            pltpu.VMEM((4, 2, 8, 3 * WIDE), jnp.float32),
            pltpu.VMEM((4, groups, LANES), jnp.float32),
            pltpu.VMEM((8, LANES), jnp.float32),
            pltpu.VMEM((8, LANES), jnp.float32),
            dma((groups,)), dma((groups,)),
            dma((half_groups,)), dma((half_groups,)),
            dma((half_groups,)), dma((half_groups,)),
            dma((half_groups,)), dma((half_groups,)),
            dma((2,)), dma((2,)),
            pltpu.VMEM((tiles, LANES), jnp.int32),
            pltpu.SMEM((1, groups), jnp.int32),
            pltpu.SMEM((1, 1), jnp.float32),
            pltpu.VMEM((2, column_width), jnp.float32),
            pltpu.VMEM((2, column_width), jnp.int32),
            pltpu.VMEM(mode_rows.shape, jnp.float32),
            pltpu.VMEM(adj_rows.shape, jnp.float32),
            pltpu.VMEM((24, 24), jnp.float32),
            pltpu.VMEM((24, 24), jnp.float32),
            pltpu.VMEM((3, 24, 24), jnp.float32),
            pltpu.VMEM((3, 24), jnp.float32),
            dma((11,)),
        ],
        compiler_params=pltpu.CompilerParams(
            vmem_limit_bytes=60 * 1024 * 1024, collective_id=0, has_side_effects=True
        ),
    )(
        node_slot.reshape(tiles, LANES), panel_spans, load_factor.reshape(1, 1), thickness, weld_land,
        mode_rows, adj_rows, membrane, bending, geometric, stress_map,
    )
    return pl.pallas_call(
        unpack_kernel,
        out_shape=(
            jax.ShapeDtypeStruct((6, 2, WIDE), jnp.float32),
            jax.ShapeDtypeStruct((2, MOST), jnp.float32),
        ),
        in_specs=[vmem],
        out_specs=(vmem, vmem),
    )(packed)


def solution(mesh):
    return jax.shard_map(
        on_device,
        mesh=mesh,
        in_specs=(
            P(None, "circ", "mer"),
            P(None, None, "circ", None),
            P(),
            P("circ", None),
            P("circ", None),
            P("circ", None),
            P(),
            P(),
            P(),
            P(),
            P(),
        ),
        out_specs=(P(None, "circ", "mer"), P("circ", "mer")),
        check_vma=False,
    )
```
